256 devices in a mesh: mem: 8 (over y, x_hi), space: 32 (over x_lo, z, core).
Axes of the slice: x: 4 (x_hi: 2, x_lo: 2; x = x_hi * 2 + x_lo), y: 4, z: 8, core: 2. Of those that a mesh axis runs over, the one named last changes fastest.
Arguments:
- ens_pert: bfloat16 [80, 127, 65536], P('mem', None, 'space'), may hold values from -6 to 6
- vert_modes: bfloat16 [127, 40], replicated, may hold values from -0.5 to 0.5
- loc_stencil: bfloat16 [1152, 65536], P(None, 'space'), may hold values from -0.1875 to 0.1875
- grad_hi: float32 [127, 262144], P(None, ('mem', 'space')), may hold values from -6 to 6
- child_map: int32 [4, 65536], P(None, 'space'), may hold values from 0 to 8191, as said below
- halo_rows: int32 [2, 32], P(None, 'space'), may hold values from 256 to 512
Outputs:
- control_grad: float32 [80, 40, 65536], P('mem', None, 'space')
The draws below stay inside these ranges and needn't reach their ends.
Inputs may be any that keep to these rules, and one draw needn't show every extreme that they name: `child_map`: within the 2048 cells of each block, the 8192 codes are each value of the range exactly once.
All inputs are finite; a program needn't handle non-finite values.
Results may differ from the reference program's by a relative error of at most 0.0065.
Values may be sent and summed in bfloat16 or wider, within the bound.
A program may use at most 128 MiB of HBM per device.

```python
import jax
import jax.numpy as jnp
from jax import lax

LEV = 127
MODES = 40
CELL_DEV = 2048
TILE = 128
HALO = 512
MEMBERS = 80
LO_CELLS = 65536
HI_CELLS = 262144
STENCIL = 1152
N_MEM = 8
N_SPACE = 32


def draw_child_map(key, part):
    key = jax.random.fold_in(key, 3)
    block_keys = jax.random.split(key, N_SPACE)
    orders = jax.vmap(lambda block_key: jax.random.permutation(block_key, 4 * CELL_DEV))(block_keys)
    return orders.reshape(N_SPACE, 4, CELL_DEV).transpose(1, 0, 2).reshape(4, N_SPACE * CELL_DEV).astype(jnp.int32)


def draw_halo_rows(key, part):
    key = jax.random.fold_in(key, 7)
    count_key, pick_key = jax.random.split(key)
    counts = jax.random.randint(count_key, (2, N_SPACE), HALO // 2, HALO + 1)
    chosen = jax.random.randint(pick_key, (), 0, 2 * N_SPACE)
    places = jnp.arange(2 * N_SPACE).reshape(2, N_SPACE)
    return jnp.where(places == chosen, HALO, counts).astype(jnp.int32)


def block_levels(key, shape, cuts, low, top_value):
    def one(axis_at, blocks):
        draws = jax.random.uniform(jax.random.fold_in(jax.random.fold_in(key, 6), axis_at), (blocks,), jnp.float32, low / len(cuts), top_value / len(cuts))
        return jnp.repeat(jnp.exp(draws), shape[axis_at] // blocks).reshape((-1,) + (1,) * (len(shape) - axis_at - 1))

    gain = one(*cuts[0])
    for cut in cuts[1:]:
        gain = gain * one(*cut)
    return gain


def gaussian(key, dims, deviation, bound, pieces=(), kind=jnp.bfloat16):
    array = deviation * jax.random.normal(key, dims, jnp.float32)
    if pieces:
        array = array * block_levels(key, dims, pieces, -0.22, 0.18)
    return jnp.clip(array, -bound, bound).astype(kind)


def setup_inputs(seed: int = 0) -> dict:
    streams_of = jax.random.split(jax.random.key(seed), 7)
    return {
        "ens_pert": gaussian(streams_of[0], (MEMBERS, LEV, LO_CELLS), 1.0, 6.0, ((0, 8), (2, 32))),
        "vert_modes": gaussian(streams_of[1], (LEV, MODES), LEV ** -0.5, 0.5),
        "loc_stencil": gaussian(streams_of[2], (STENCIL, LO_CELLS), STENCIL ** -0.5, 0.1875, ((1, 32),)),
        "grad_hi": gaussian(streams_of[3], (LEV, HI_CELLS), 1.0, 6.0, ((1, 256),), jnp.float32),
        "child_map": draw_child_map(jax.random.fold_in(streams_of[6], 71), 0),
        "halo_rows": draw_halo_rows(jax.random.fold_in(streams_of[6], 71), 0),
    }


def reference(ens_pert, vert_modes, loc_stencil, grad_hi, child_map, halo_rows):
    hi_dev = 4 * CELL_DEV // N_MEM
    send_rows = hi_dev // N_SPACE
    owner_block = jnp.arange(LO_CELLS, dtype=jnp.int32) // CELL_DEV
    source_mem = child_map // hi_dev
    placed = child_map % hi_dev
    hi_column = (source_mem * N_SPACE + placed // send_rows) * hi_dev + owner_block[None, :] * send_rows + placed % send_rows
    picked = jnp.take(grad_hi, hi_column.reshape(-1).astype(jnp.int32), axis=1).reshape(LEV, 4, LO_CELLS)
    coarse = 0.25 * jnp.sum(picked, axis=1)
    modes_wide = vert_modes.astype(jnp.float32)

    def member_modes(member_pert):
        product = (member_pert.astype(jnp.float32) * coarse).astype(jnp.bfloat16)
        return jnp.dot(modes_wide.T, product.astype(jnp.float32), precision=lax.Precision.HIGHEST)

    reduced = lax.map(member_modes, ens_pert)
    span_cols = CELL_DEV + 2 * HALO
    tile_count = CELL_DEV // TILE
    positions = jnp.arange(span_cols, dtype=jnp.int32)

    def one_block(block_number):
        first_cell = block_number * CELL_DEV - HALO
        cell_index = ((first_cell + positions) % LO_CELLS).astype(jnp.int32)
        kept_cols = (positions >= HALO - halo_rows[0, block_number]) & (positions < HALO + CELL_DEV + halo_rows[1, block_number])
        window = jnp.where(kept_cols[None, None, :], jnp.take(reduced, cell_index, axis=2), jnp.float32(0.0))
        stencil = lax.dynamic_slice_in_dim(loc_stencil, (block_number * CELL_DEV).astype(jnp.int32), CELL_DEV, 1).astype(jnp.float32)

        def one_tile(tile_number):
            window_part = lax.dynamic_slice_in_dim(window, (tile_number * TILE).astype(jnp.int32), TILE + 2 * HALO, 2)
            weights = lax.dynamic_slice_in_dim(stencil, (tile_number * TILE).astype(jnp.int32), TILE, 1)
            return jnp.einsum("kmi,ij->kmj", window_part, weights, precision=lax.Precision.HIGHEST)

        tile_results = lax.map(one_tile, jnp.arange(tile_count, dtype=jnp.int32))
        return tile_results.transpose(1, 2, 0, 3).reshape(MEMBERS, MODES, CELL_DEV)

    block_results = lax.map(one_block, jnp.arange(N_SPACE, dtype=jnp.int32))
    return block_results.transpose(1, 2, 0, 3).reshape(MEMBERS, MODES, LO_CELLS)
```

```python
import jax
import jax.numpy as jnp
from jax import lax
from jax.experimental import pallas as pl
from jax.experimental.pallas import tpu as pltpu
from jax.sharding import PartitionSpec as P

MESH = pl.DeviceIdType.MESH
BF16 = jnp.bfloat16
F32 = jnp.float32

TILE = 128
HALO = 512
LEV = 127
LEV_PAD = 128
MODES = 40
CELLS = 2048
EXT = CELLS + 2 * HALO
N_MEM = 8
N_SPACE = 32
CHUNK = LEV_PAD // N_MEM
HI = 1024
SEND = HI // N_SPACE
CODES = 512
GROUPS = N_MEM * HI // CODES
EDGE = 2 * HALO
PAIRS = 5
ROWS = 2 * MODES


def remote(src, dst, send, recv, mem, space):
    return pltpu.make_async_remote_copy(
        src_ref=src,
        dst_ref=dst,
        send_sem=send,
        recv_sem=recv,
        device_id=(mem, space),
        device_id_type=MESH,
    )


def reduce_kernel(
    grad, child, modes, ens_hbm, out_hbm,
    gb, got_levels, turned, got_cols, picker, coarse_edge, coarse_mid, ens, prod, modes_pad, modes_two, red,
    ens_sem, m_send, m_recv, s_send, s_recv, e_send, e_recv, c_send, c_recv, h_send, h_recv, out_sem,
):
    mem = lax.axis_index("mem")
    space = lax.axis_index("space")
    mem_at = lambda d: lax.rem(mem + d, N_MEM)
    space_at = lambda d: lax.rem(space + d, N_SPACE)

    ens_copy = pltpu.make_async_copy(ens_hbm, ens, ens_sem)
    ens_copy.start()

    barrier = pltpu.get_barrier_semaphore()

    @pl.loop(1, N_MEM)
    def _(d):
        pl.semaphore_signal(barrier, inc=1, device_id=(mem_at(d), space), device_id_type=MESH)

    @pl.loop(1, N_SPACE)
    def _(d):
        pl.semaphore_signal(barrier, inc=1, device_id=(mem, space_at(d)), device_id_type=MESH)

    for m in range(N_MEM - 1):
        gb[m] = grad[m * CHUNK : (m + 1) * CHUNK, :].astype(BF16)
    last = grad[(N_MEM - 1) * CHUNK : LEV, :]
    gb[N_MEM - 1] = jnp.concatenate([last, jnp.zeros((1, HI), F32)], axis=0).astype(BF16)

    pl.semaphore_wait(barrier, N_MEM - 1 + N_SPACE - 1)

    def level_copy(d):
        target = mem_at(d)
        return remote(gb.at[target], got_levels.at[mem], m_send.at[d], m_recv.at[d], target, space)

    @pl.loop(1, N_MEM)
    def _(d):
        level_copy(d).start()

    got_levels[mem] = gb[mem]

    modes_pad[...] = jnp.zeros_like(modes_pad)
    modes_pad[0:LEV, 0:MODES] = modes[...].astype(F32)
    flipped = modes_pad[...].T[0:MODES, :]
    modes_two[...] = jnp.zeros_like(modes_two)
    modes_two[0:MODES, 0:LEV_PAD] = flipped
    modes_two[MODES:ROWS, LEV_PAD : 2 * LEV_PAD] = flipped
    prod[...] = jnp.zeros_like(prod)

    @pl.loop(1, N_MEM)
    def _(d):
        level_copy(d).wait()

    for q in range(HI // 128):
        part = got_levels[:, :, q * 128 : (q + 1) * 128].reshape(LEV_PAD, 128)
        turned[q * 4 : (q + 1) * 4] = part.T.reshape(4, SEND, LEV_PAD)

    def column_copy(d):
        target = space_at(d)
        return remote(turned.at[target], got_cols.at[space], s_send.at[d], s_recv.at[d], mem, target)

    @pl.loop(1, N_SPACE)
    def _(d):
        column_copy(d).start()

    got_cols[space] = turned[space]

    @pl.loop(0, 4 * CELLS // 256)
    def _(t):
        j = t // (CELLS // 256)
        first = pl.multiple_of(lax.rem(t, CELLS // 256) * 256, 256)
        low = child[pl.ds(j, 1), pl.ds(first, 256)] & (CODES - 1)
        hot = lax.broadcasted_iota(jnp.int32, (CODES, 256), 0) == low
        picker[:, pl.ds(pl.multiple_of(t * 256, 256), 256)] = hot.astype(F32).astype(BF16)

    @pl.loop(1, N_SPACE)
    def _(d):
        column_copy(d).wait()

    halves = []
    for h in range(2):
        cols = got_cols[h * 16 : (h + 1) * 16].reshape(CODES, LEV_PAD)
        halves.append(cols.T)
    table = jnp.concatenate(halves, axis=0)

    def pick(first, width):
        total = jnp.zeros((CHUNK, width), F32)
        for j in range(4):
            found = jnp.dot(
                table, picker[:, j * CELLS + first : j * CELLS + first + width], preferred_element_type=F32
            )
            code = child[j : j + 1, first : first + width]
            group = ((code >> 9) & 1) * N_MEM + (code >> 10)
            for g in range(GROUPS):
                total = total + jnp.where(group == g, found[g * CHUNK : (g + 1) * CHUNK, :], 0.0)
        return (0.25 * total).astype(BF16)

    def edge_copy(d):
        return remote(coarse_edge.at[mem], coarse_edge.at[mem], e_send.at[d], e_recv.at[d], mem_at(d), space)

    def mid_copy(d):
        return remote(coarse_mid.at[mem], coarse_mid.at[mem], c_send.at[d], c_recv.at[d], mem_at(d), space)

    coarse_edge[mem, :, 0:HALO] = pick(0, HALO)
    coarse_edge[mem, :, HALO:EDGE] = pick(CELLS - HALO, HALO)

    @pl.loop(1, N_MEM)
    def _(d):
        edge_copy(d).start()

    coarse_mid[mem, :, 0:HALO] = pick(HALO, HALO)
    coarse_mid[mem, :, HALO:EDGE] = pick(2 * HALO, HALO)

    @pl.loop(1, N_MEM)
    def _(d):
        mid_copy(d).start()

    two = modes_two[...].astype(BF16)

    def reduced(pair, cells, coarse):
        for i in range(2):
            prod[i * LEV_PAD : i * LEV_PAD + LEV, :] = ens[2 * pair + i, :, cells : cells + HALO] * coarse
        return jnp.dot(two, prod[...], preferred_element_type=F32).astype(BF16)

    def to_lower(pair):
        rows = pl.ds(pair * ROWS, ROWS)
        return remote(
            red.at[rows, pl.ds(HALO, HALO)], red.at[rows, pl.ds(HALO + CELLS, HALO)],
            h_send.at[0, pair], h_recv.at[0, pair], mem, space_at(N_SPACE - 1),
        )

    def to_upper(pair):
        rows = pl.ds(pair * ROWS, ROWS)
        return remote(
            red.at[rows, pl.ds(CELLS, HALO)], red.at[rows, pl.ds(0, HALO)],
            h_send.at[1, pair], h_recv.at[1, pair], mem, space_at(1),
        )

    ens_copy.wait()

    @pl.loop(1, N_MEM)
    def _(d):
        edge_copy(d).wait()

    low = coarse_edge[:, :, 0:HALO].reshape(LEV_PAD, HALO)[0:LEV]
    high = coarse_edge[:, :, HALO:EDGE].reshape(LEV_PAD, HALO)[0:LEV]
    for pair in range(PAIRS):
        rows = slice(pair * ROWS, (pair + 1) * ROWS)
        red[rows, HALO : 2 * HALO] = reduced(pair, 0, low)
        to_lower(pair).start()
        red[rows, CELLS : CELLS + HALO] = reduced(pair, CELLS - HALO, high)
        to_upper(pair).start()

    @pl.loop(1, N_MEM)
    def _(d):
        mid_copy(d).wait()

    for half in range(2):
        coarse = coarse_mid[:, :, half * HALO : (half + 1) * HALO].reshape(LEV_PAD, HALO)[0:LEV]
        cells = HALO * (1 + half)
        for pair in range(PAIRS):
            red[pair * ROWS : (pair + 1) * ROWS, HALO + cells : 2 * HALO + cells] = reduced(pair, cells, coarse)

    def out_copy(i, first, width):
        return pltpu.make_async_copy(
            red.at[:, pl.ds(first, width)], out_hbm.at[:, pl.ds(first, width)], out_sem.at[i]
        )

    copies = [out_copy(0, HALO, CELLS), out_copy(1, 0, HALO), out_copy(2, HALO + CELLS, HALO)]
    copies[0].start()
    for pair in range(PAIRS):
        to_lower(pair).wait()
        to_upper(pair).wait()
    copies[1].start()
    copies[2].start()
    for copy in copies:
        copy.wait()


def smooth_kernel(halo_rows, ext, stencil, out, window, weights, sems):
    t = pl.program_id(0)
    span = 2 * TILE + 2 * HALO

    def load(tile, side):
        return pltpu.make_async_copy(
            stencil.at[:, pl.ds(tile * 2 * TILE + side * TILE, TILE)],
            weights.at[tile, pl.ds(side * TILE, TILE + 2 * HALO), pl.ds(side * TILE, TILE)],
            sems.at[tile, side],
        )

    @pl.when(t == 0)
    def _():
        for tile in range(CELLS // (2 * TILE)):
            for side in range(2):
                load(tile, side).start()
        for tile in range(CELLS // (2 * TILE)):
            weights[tile, span - TILE : span, 0:TILE] = jnp.zeros((TILE, TILE), BF16)
            weights[tile, 0:TILE, TILE : 2 * TILE] = jnp.zeros((TILE, TILE), BF16)
        col = lax.broadcasted_iota(jnp.int32, (5 * ROWS, HALO), 1)
        window[:, HALO : HALO + CELLS] = ext[:, HALO : HALO + CELLS]
        low = ext[:, 0:HALO].astype(F32)
        window[:, 0:HALO] = jnp.where(col >= HALO - halo_rows[0, 0], low, 0.0).astype(BF16)
        high = ext[:, HALO + CELLS : EXT].astype(F32)
        window[:, HALO + CELLS : EXT] = jnp.where(col < halo_rows[1, 0], high, 0.0).astype(BF16)

    load(t, 0).wait()
    load(t, 1).wait()
    first = pl.multiple_of(t * 2 * TILE, 2 * TILE)
    out[...] = jnp.dot(window[:, pl.ds(first, span)], weights[t], preferred_element_type=F32)


def local(ens_pert, vert_modes, loc_stencil, grad_hi, child_map, halo_rows):
    vmem = pl.BlockSpec(memory_space=pltpu.VMEM)
    anywhere = pl.BlockSpec(memory_space=pl.ANY)
    dma = pltpu.SemaphoreType.DMA
    rows = PAIRS * ROWS
    ext = pl.pallas_call(
        reduce_kernel,
        out_shape=jax.ShapeDtypeStruct((rows, EXT), BF16),
        in_specs=[vmem, vmem, vmem, anywhere],
        out_specs=anywhere,
        scratch_shapes=[
            pltpu.VMEM((N_MEM, CHUNK, HI), BF16),
            pltpu.VMEM((N_MEM, CHUNK, HI), BF16),
            pltpu.VMEM((N_SPACE, SEND, LEV_PAD), BF16),
            pltpu.VMEM((N_SPACE, SEND, LEV_PAD), BF16),
            pltpu.VMEM((CODES, 4 * CELLS), BF16),
            pltpu.VMEM((N_MEM, CHUNK, EDGE), BF16),
            pltpu.VMEM((N_MEM, CHUNK, EDGE), BF16),
            pltpu.VMEM((2 * PAIRS, LEV, CELLS), BF16),
            pltpu.VMEM((2 * LEV_PAD, HALO), BF16),
            pltpu.VMEM((LEV_PAD, 128), F32),
            pltpu.VMEM((ROWS, 2 * LEV_PAD), F32),
            pltpu.VMEM((rows, EXT), BF16),
            dma,
            dma((N_MEM,)),
            dma((N_MEM,)),
            dma((N_SPACE,)),
            dma((N_SPACE,)),
            dma((N_MEM,)),
            dma((N_MEM,)),
            dma((N_MEM,)),
            dma((N_MEM,)),
            dma((2, PAIRS)),
            dma((2, PAIRS)),
            dma((3,)),
        ],
        compiler_params=pltpu.CompilerParams(
            collective_id=0, has_side_effects=True, vmem_limit_bytes=40 * 2**20
        ),
        name="reduce",
    )(grad_hi, child_map, vert_modes, ens_pert)

    out = pl.pallas_call(
        smooth_kernel,
        grid=(CELLS // (2 * TILE),),
        out_shape=jax.ShapeDtypeStruct((rows, CELLS), F32),
        in_specs=[
            pl.BlockSpec(memory_space=pltpu.SMEM),
            vmem,
            anywhere,
        ],
        out_specs=pl.BlockSpec((rows, 2 * TILE), lambda t: (0, t)),
        scratch_shapes=[
            pltpu.VMEM((rows, EXT), BF16),
            pltpu.VMEM((CELLS // (2 * TILE), 2 * TILE + 2 * HALO, 2 * TILE), BF16),
            dma((CELLS // (2 * TILE), 2)),
        ],
        compiler_params=pltpu.CompilerParams(vmem_limit_bytes=40 * 2**20),
        name="smooth",
    )(halo_rows, ext, loc_stencil)
    return out.reshape(2 * PAIRS, MODES, CELLS)


def solution(mesh):
    placed = (
        P("mem", None, "space"),
        P(),
        P(None, "space"),
        P(None, ("mem", "space")),
        P(None, "space"),
        P(None, "space"),
    )
    return jax.shard_map(
        local, mesh=mesh, in_specs=placed, out_specs=P("mem", None, "space"), check_vma=False
    )
```

```python
import jax
import jax.numpy as jnp
from jax import lax
from jax.experimental import pallas as pl
from jax.experimental.pallas import tpu as pltpu
from jax.sharding import PartitionSpec as P

MESH = pl.DeviceIdType.MESH
BF16 = jnp.bfloat16
F32 = jnp.float32

TILE = 128
HALO = 512
LEV = 127
LEV_PAD = 128
MODES = 40
CELLS = 2048
EXT = CELLS + 2 * HALO
N_MEM = 8
N_SPACE = 32
CHUNK = LEV_PAD // N_MEM
HI = 1024
SEND = HI // N_SPACE
CODES = 512
GROUPS = N_MEM * HI // CODES
PAIRS = 5
ROWS = 2 * MODES
ALL_ROWS = PAIRS * ROWS
MID = CELLS - 2 * HALO
PART = 2 * TILE
SPAN = PART + 2 * HALO

MEM_STEPS = ((2, 1), (1, 1), (3, 1), (0, 1), (2, 0), (1, 0), (3, 0))
Z_STEPS = (4, 3, 5, 2, 6, 1, 7, 0)
OWN_STEPS = [(z, c) for z in Z_STEPS for c in (1, 0) if z or c]
OTHER_STEPS = [(z, c) for z in Z_STEPS for c in (1, 0)]


def remote(src, dst, send, recv, mem, space):
    return pltpu.make_async_remote_copy(
        src_ref=src,
        dst_ref=dst,
        send_sem=send,
        recv_sem=recv,
        device_id=(mem, space),
        device_id_type=MESH,
    )


def paired(even, odd):
    blank = jnp.zeros((TILE, TILE), even.dtype)
    return jnp.concatenate(
        [jnp.concatenate([even, blank], axis=0), jnp.concatenate([blank, odd], axis=0)], axis=1
    )


def reduce_kernel(
    grad_hbm, child_hbm, modes_hbm, ens_hbm, stencil_hbm, red, mid_out,
    grad, child, modes, ens, stencil, gb, got_levels, turned, got_cols, table, picker,
    coarse_far, coarse_rest, prod, modes_two,
    in_sem, m_send, m_recv, s_send, s_recv, e_send, e_recv, c_send, c_recv, h_send, h_recv,
):
    mem = lax.axis_index("mem")
    space = lax.axis_index("space")
    y, x_hi = mem // 2, lax.rem(mem, 2)
    x_lo, z, core = space // 16, lax.rem(space // 2, 8), lax.rem(space, 2)

    def mem_at(step):
        return lax.rem(y + step[0], 4) * 2 + lax.rem(x_hi + step[1], 2)

    def space_at(x, step):
        return x * 16 + lax.rem(z + step[0], 8) * 2 + lax.rem(core + step[1], 2)

    loads = [
        pltpu.make_async_copy(src, dst, in_sem.at[i])
        for i, (src, dst) in enumerate(
            (
                (grad_hbm, grad),
                (modes_hbm, modes),
                (child_hbm, child),
                (ens_hbm, ens),
                (stencil_hbm.at[:, pl.ds(HALO, MID)], stencil),
            )
        )
    ]
    for load in loads:
        load.start()

    barrier = pltpu.get_barrier_semaphore()
    for step in OTHER_STEPS:
        pl.semaphore_signal(barrier, inc=1, device_id=(mem, space_at(1 - x_lo, step)), device_id_type=MESH)
    for step in MEM_STEPS:
        pl.semaphore_signal(barrier, inc=1, device_id=(mem_at(step), space), device_id_type=MESH)
    for step in OWN_STEPS:
        pl.semaphore_signal(barrier, inc=1, device_id=(mem, space_at(x_lo, step)), device_id_type=MESH)

    loads[0].wait()
    for m in range(N_MEM - 1):
        gb[m] = grad[m * CHUNK : (m + 1) * CHUNK, :].astype(BF16)
    last = grad[(N_MEM - 1) * CHUNK : LEV, :]
    gb[N_MEM - 1] = jnp.concatenate([last, jnp.zeros((1, HI), F32)], axis=0).astype(BF16)

    pl.semaphore_wait(barrier, N_MEM - 1 + N_SPACE - 1)

    sides = (x_lo, 1 - x_lo)

    def level_copy(k, i):
        target = mem_at(MEM_STEPS[i])
        cols = pl.ds(pl.multiple_of(sides[k] * CODES, CODES), CODES)
        return remote(
            gb.at[target, :, cols], got_levels.at[mem, :, cols], m_send.at[k, i], m_recv.at[k, i], target, space
        )

    for k in range(2):
        for i in range(N_MEM - 1):
            level_copy(k, i).start()

    got_levels[mem] = gb[mem]

    loads[1].wait()
    modes_two[...] = jnp.zeros_like(modes_two)
    wide = modes[...].astype(F32)
    modes_two[0:MODES, 0:LEV] = wide
    modes_two[MODES:ROWS, LEV_PAD : LEV_PAD + LEV] = wide
    prod[...] = jnp.zeros_like(prod)

    def column_copy(k, i):
        target = space_at(sides[k], (OWN_STEPS, OTHER_STEPS)[k][i])
        return remote(turned.at[target], got_cols.at[space], s_send.at[k, i], s_recv.at[k, i], mem, target)

    counts = (len(OWN_STEPS), len(OTHER_STEPS))
    for k in range(2):
        for i in range(N_MEM - 1):
            level_copy(k, i).wait()
        for q in range(CODES // 128):
            first = pl.multiple_of(sides[k] * CODES + q * 128, 128)
            part = got_levels[:, :, pl.ds(first, 128)].reshape(LEV_PAD, 128)
            turned[pl.ds(sides[k] * 16 + q * 4, 4)] = part.T.reshape(4, SEND, LEV_PAD)
        for i in range(counts[k]):
            column_copy(k, i).start()

    got_cols[space] = turned[space]
    loads[2].wait()

    @pl.loop(0, 4 * CELLS // 256)
    def _(t):
        j = t // (CELLS // 256)
        first = pl.multiple_of(lax.rem(t, CELLS // 256) * 256, 256)
        low = child[pl.ds(j, 1), pl.ds(first, 256)] & (CODES - 1)
        hot = lax.broadcasted_iota(jnp.int32, (CODES, 256), 0) == low
        picker[:, pl.ds(pl.multiple_of(t * 256, 256), 256)] = hot.astype(F32).astype(BF16)

    for k in range(2):
        for i in range(counts[k]):
            column_copy(k, i).wait()
        cols = got_cols[pl.ds(sides[k] * 16, 16)].reshape(CODES, LEV_PAD)
        table[pl.ds(pl.multiple_of(sides[k] * LEV_PAD, LEV_PAD), LEV_PAD), :] = cols.T

    def pick(first, width):
        total = jnp.zeros((CHUNK, width), F32)
        for j in range(4):
            cells = pl.ds(pl.multiple_of(j * CELLS + first, HALO), width)
            found = jnp.dot(table[...], picker[:, cells], preferred_element_type=F32)
            code = child[j : j + 1, pl.ds(pl.multiple_of(first, HALO), width)]
            group = ((code >> 9) & 1) * N_MEM + (code >> 10)
            for g in range(GROUPS):
                total = total + jnp.where(group == g, found[g * CHUNK : (g + 1) * CHUNK, :], 0.0)
        return (0.25 * total).astype(BF16)

    def far_copy(i):
        return remote(
            coarse_far.at[mem], coarse_far.at[mem], e_send.at[i], e_recv.at[i], mem_at(MEM_STEPS[i]), space
        )

    def rest_copy(i):
        return remote(
            coarse_rest.at[mem], coarse_rest.at[mem], c_send.at[i], c_recv.at[i], mem_at(MEM_STEPS[i]), space
        )

    far = core * (CELLS - HALO)
    near = (1 - core) * (CELLS - HALO)
    coarse_far[mem] = pick(far, HALO)
    for i in range(N_MEM - 1):
        far_copy(i).start()
    coarse_rest[mem, :, 0:HALO] = pick(near, HALO)
    coarse_rest[mem, :, HALO : 2 * HALO] = pick(HALO, HALO)
    coarse_rest[mem, :, 2 * HALO : 3 * HALO] = pick(2 * HALO, HALO)
    for i in range(N_MEM - 1):
        rest_copy(i).start()

    two = modes_two[...].astype(BF16)

    def reduce_cells(pair, first, coarse):
        for i in range(2):
            pert = ens[2 * pair + i, :, pl.ds(pl.multiple_of(first, HALO), HALO)]
            prod[i * LEV_PAD : i * LEV_PAD + LEV, :] = pert * coarse
        value = jnp.dot(two, prod[...], preferred_element_type=F32).astype(BF16)
        red[pair * ROWS : (pair + 1) * ROWS, pl.ds(pl.multiple_of(HALO + first, HALO), HALO)] = value

    def halo_copy(side, pair):
        rows = pl.ds(pair * ROWS, ROWS)
        first, place, target = (
            (far, (1 - core) * (HALO + CELLS), lax.rem(space + 2 * core + N_SPACE - 1, N_SPACE)),
            (near, core * (HALO + CELLS), space + 1 - 2 * core),
        )[side]
        return remote(
            red.at[rows, pl.ds(pl.multiple_of(HALO + first, HALO), HALO)],
            red.at[rows, pl.ds(pl.multiple_of(place, HALO), HALO)],
            h_send.at[side, pair], h_recv.at[side, pair], mem, target,
        )

    loads[3].wait()
    for i in range(N_MEM - 1):
        far_copy(i).wait()
    coarse = coarse_far[...].reshape(LEV_PAD, HALO)[0:LEV]
    for pair in range(PAIRS):
        reduce_cells(pair, far, coarse)
        halo_copy(0, pair).start()

    for i in range(N_MEM - 1):
        rest_copy(i).wait()
    coarse = coarse_rest[:, :, 0:HALO].reshape(LEV_PAD, HALO)[0:LEV]
    for pair in range(PAIRS):
        reduce_cells(pair, near, coarse)
        halo_copy(1, pair).start()
    for half in range(2):
        coarse = coarse_rest[:, :, (half + 1) * HALO : (half + 2) * HALO].reshape(LEV_PAD, HALO)[0:LEV]
        for pair in range(PAIRS):
            reduce_cells(pair, HALO * (half + 1), coarse)

    loads[4].wait()
    for part in range(MID // PART):
        cells = part * PART
        weights = paired(stencil[:, cells : cells + TILE], stencil[:, cells + TILE : cells + PART])
        window = red[:, HALO + cells : HALO + cells + SPAN]
        mid_out[:, cells : cells + PART] = jnp.dot(window, weights, preferred_element_type=F32)

    for side in range(2):
        for pair in range(PAIRS):
            halo_copy(side, pair).wait()


def edge_kernel(halo_rows, ext, stencil, mid, out, result, sems):
    mid_copy = pltpu.make_async_copy(mid, out.at[:, pl.ds(HALO, MID)], sems.at[0])
    mid_copy.start()
    copies = [mid_copy]

    col = lax.broadcasted_iota(jnp.int32, (16, HALO), 1)
    low_kept = (col >= HALO - halo_rows[0, 0]).astype(F32).astype(BF16)[0:1]
    high_kept = (col < halo_rows[0, 1]).astype(F32).astype(BF16)[0:1]
    low = ext[:, 0:HALO] * low_kept
    high = ext[:, HALO + CELLS : EXT] * high_kept

    for n, part in enumerate((0, 1, CELLS // PART - 2, CELLS // PART - 1)):
        cells = part * PART
        if part < 2:
            window = jnp.concatenate([low[:, cells:], ext[:, HALO : cells + SPAN]], axis=1)
        else:
            window = jnp.concatenate(
                [ext[:, cells : HALO + CELLS], high[:, 0 : cells + SPAN - HALO - CELLS]], axis=1
            )
        weights = paired(stencil[:, cells : cells + TILE], stencil[:, cells + TILE : cells + PART])
        result[n] = jnp.dot(window, weights, preferred_element_type=F32)
        copy = pltpu.make_async_copy(result.at[n], out.at[:, pl.ds(cells, PART)], sems.at[n + 1])
        copy.start()
        copies.append(copy)
    for copy in copies:
        copy.wait()


def local(ens_pert, vert_modes, loc_stencil, grad_hi, child_map, halo_rows):
    vmem = pl.BlockSpec(memory_space=pltpu.VMEM)
    hbm = pl.BlockSpec(memory_space=pltpu.HBM)
    anywhere = pl.BlockSpec(memory_space=pl.ANY)
    dma = pltpu.SemaphoreType.DMA
    held = [
        pltpu.with_memory_space_constraint(x, pltpu.HBM)
        for x in (grad_hi, child_map, vert_modes.T, ens_pert, loc_stencil)
    ]
    ext, mid = pl.pallas_call(
        reduce_kernel,
        out_shape=(
            jax.ShapeDtypeStruct((ALL_ROWS, EXT), BF16),
            jax.ShapeDtypeStruct((ALL_ROWS, MID), F32),
        ),
        in_specs=[hbm] * 5,
        out_specs=(vmem, vmem),
        scratch_shapes=[
            pltpu.VMEM((LEV, HI), F32),
            pltpu.VMEM((4, CELLS), jnp.int32),
            pltpu.VMEM((MODES, LEV), BF16),
            pltpu.VMEM((2 * PAIRS, LEV, CELLS), BF16),
            pltpu.VMEM((TILE + 2 * HALO, MID), BF16),
            pltpu.VMEM((N_MEM, CHUNK, HI), BF16),
            pltpu.VMEM((N_MEM, CHUNK, HI), BF16),
            pltpu.VMEM((N_SPACE, SEND, LEV_PAD), BF16),
            pltpu.VMEM((N_SPACE, SEND, LEV_PAD), BF16),
            pltpu.VMEM((2 * LEV_PAD, CODES), BF16),
            pltpu.VMEM((CODES, 4 * CELLS), BF16),
            pltpu.VMEM((N_MEM, CHUNK, HALO), BF16),
            pltpu.VMEM((N_MEM, CHUNK, 3 * HALO), BF16),
            pltpu.VMEM((2 * LEV_PAD, HALO), BF16),
            pltpu.VMEM((ROWS, 2 * LEV_PAD), F32),
            dma((5,)),
            dma((2, N_MEM)),
            dma((2, N_MEM)),
            dma((2, N_SPACE // 2)),
            dma((2, N_SPACE // 2)),
            dma((N_MEM,)),
            dma((N_MEM,)),
            dma((N_MEM,)),
            dma((N_MEM,)),
            dma((2, PAIRS)),
            dma((2, PAIRS)),
        ],
        compiler_params=pltpu.CompilerParams(
            collective_id=0, has_side_effects=True, vmem_limit_bytes=40 * 2**20
        ),
        name="reduce",
    )(*held)

    out = pl.pallas_call(
        edge_kernel,
        out_shape=jax.ShapeDtypeStruct((ALL_ROWS, CELLS), F32),
        in_specs=[pl.BlockSpec(memory_space=pltpu.SMEM), vmem, vmem, anywhere],
        out_specs=anywhere,
        scratch_shapes=[pltpu.VMEM((4, ALL_ROWS, PART), F32), dma((5,))],
        compiler_params=pltpu.CompilerParams(vmem_limit_bytes=40 * 2**20),
        name="edges",
    )(halo_rows.T, ext, loc_stencil, mid)
    return out.reshape(2 * PAIRS, MODES, CELLS)


def solution(mesh):
    placed = (
        P("mem", None, "space"),
        P(),
        P(None, "space"),
        P(None, ("mem", "space")),
        P(None, "space"),
        P(None, "space"),
    )
    return jax.shard_map(
        local, mesh=mesh, in_specs=placed, out_specs=P("mem", None, "space"), check_vma=False
    )
```

```python
import jax
import jax.numpy as jnp
from jax import lax
from jax.experimental import pallas as pl
from jax.experimental.pallas import tpu as pltpu
from jax.sharding import PartitionSpec as P

MESH = pl.DeviceIdType.MESH
BF16 = jnp.bfloat16
F32 = jnp.float32

TILE = 128
HALO = 512
LEV = 127
LEV_PAD = 128
MODES = 40
CELLS = 2048
EXT = CELLS + 2 * HALO
N_MEM = 8
N_SPACE = 32
CHUNK = LEV_PAD // N_MEM
HI = 1024
SEND = HI // N_SPACE
CODES = 512
GROUPS = N_MEM * HI // CODES
PAIRS = 5
ROWS = 2 * MODES
ALL_ROWS = PAIRS * ROWS
MID = CELLS - 2 * HALO
PART = 2 * TILE
SPAN = PART + 2 * HALO

MEM_STEPS = ((2, 1), (1, 1), (3, 1), (0, 1), (2, 0), (1, 0), (3, 0))
Z_STEPS = (4, 3, 5, 2, 6, 1, 7, 0)
OWN_STEPS = [(z, c) for z in Z_STEPS for c in (1, 0) if z or c]
OTHER_STEPS = [(z, c) for z in Z_STEPS for c in (1, 0)]


def remote(src, dst, send, recv, mem, space):
    return pltpu.make_async_remote_copy(
        src_ref=src,
        dst_ref=dst,
        send_sem=send,
        recv_sem=recv,
        device_id=(mem, space),
        device_id_type=MESH,
    )


def paired(even, odd):
    blank = jnp.zeros((TILE, TILE), even.dtype)
    return jnp.concatenate(
        [jnp.concatenate([even, blank], axis=0), jnp.concatenate([blank, odd], axis=0)], axis=1
    )


def reduce_kernel(
    grad_hbm, child_hbm, modes_hbm, ens_hbm, stencil_hbm, red, mid_out,
    grad, child, modes, ens, stencil, gb, got_levels, turned, got_cols, table, picker,
    coarse_far, coarse_rest, prod, modes_two,
    in_sem, m_send, m_recv, s_send, s_recv, e_send, e_recv, c_send, c_recv, h_send, h_recv,
):
    mem = lax.axis_index("mem")
    space = lax.axis_index("space")
    y, x_hi = mem // 2, lax.rem(mem, 2)
    x_lo, z, core = space // 16, lax.rem(space // 2, 8), lax.rem(space, 2)

    def mem_at(step):
        return lax.rem(y + step[0], 4) * 2 + lax.rem(x_hi + step[1], 2)

    def space_at(x, step):
        return x * 16 + lax.rem(z + step[0], 8) * 2 + lax.rem(core + step[1], 2)

    loads = [
        pltpu.make_async_copy(src, dst, in_sem.at[i])
        for i, (src, dst) in enumerate(
            (
                (grad_hbm, grad),
                (modes_hbm, modes),
                (child_hbm, child),
                (ens_hbm, ens),
                (stencil_hbm.at[:, pl.ds(HALO, MID)], stencil),
            )
        )
    ]
    for load in loads:
        load.start()

    barrier = pltpu.get_barrier_semaphore()
    for step in OTHER_STEPS:
        pl.semaphore_signal(barrier, inc=1, device_id=(mem, space_at(1 - x_lo, step)), device_id_type=MESH)
    for step in MEM_STEPS:
        pl.semaphore_signal(barrier, inc=1, device_id=(mem_at(step), space), device_id_type=MESH)
    for step in OWN_STEPS:
        pl.semaphore_signal(barrier, inc=1, device_id=(mem, space_at(x_lo, step)), device_id_type=MESH)

    loads[0].wait()
    for m in range(N_MEM - 1):
        gb[m] = grad[m * CHUNK : (m + 1) * CHUNK, :].astype(BF16)
    last = grad[(N_MEM - 1) * CHUNK : LEV, :]
    gb[N_MEM - 1] = jnp.concatenate([last, jnp.zeros((1, HI), F32)], axis=0).astype(BF16)

    pl.semaphore_wait(barrier, N_MEM - 1 + N_SPACE - 1)

    sides = (x_lo, 1 - x_lo)

    def level_copy(k, i):
        target = mem_at(MEM_STEPS[i])
        cols = pl.ds(pl.multiple_of(sides[k] * CODES, CODES), CODES)
        return remote(
            gb.at[target, :, cols], got_levels.at[mem, :, cols], m_send.at[k, i], m_recv.at[k, i], target, space
        )

    for k in range(2):
        for i in range(N_MEM - 1):
            level_copy(k, i).start()

    got_levels[mem] = gb[mem]

    loads[1].wait()
    modes_two[...] = jnp.zeros_like(modes_two)
    wide = modes[...].astype(F32)
    modes_two[0:MODES, 0:LEV] = wide
    modes_two[MODES:ROWS, LEV_PAD : LEV_PAD + LEV] = wide
    prod[...] = jnp.zeros_like(prod)

    def column_copy(k, i):
        target = space_at(sides[k], (OWN_STEPS, OTHER_STEPS)[k][i])
        return remote(turned.at[target], got_cols.at[space], s_send.at[k, i], s_recv.at[k, i], mem, target)

    counts = (len(OWN_STEPS), len(OTHER_STEPS))
    for k in range(2):
        for i in range(N_MEM - 1):
            level_copy(k, i).wait()
        for q in range(CODES // 128):
            first = pl.multiple_of(sides[k] * CODES + q * 128, 128)
            part = got_levels[:, :, pl.ds(first, 128)].reshape(LEV_PAD, 128)
            turned[pl.ds(sides[k] * 16 + q * 4, 4)] = part.T.reshape(4, SEND, LEV_PAD)
        for i in range(counts[k]):
            column_copy(k, i).start()

    got_cols[space] = turned[space]
    loads[2].wait()

    @pl.loop(0, 4 * CELLS // 256)
    def _(t):
        j = t // (CELLS // 256)
        first = pl.multiple_of(lax.rem(t, CELLS // 256) * 256, 256)
        low = child[pl.ds(j, 1), pl.ds(first, 256)] & (CODES - 1)
        hot = lax.broadcasted_iota(jnp.int32, (CODES, 256), 0) == low
        picker[:, pl.ds(pl.multiple_of(t * 256, 256), 256)] = hot.astype(F32).astype(BF16)

    for k in range(2):
        for i in range(counts[k]):
            column_copy(k, i).wait()
        cols = got_cols[pl.ds(sides[k] * 16, 16)].reshape(CODES, LEV_PAD)
        table[pl.ds(pl.multiple_of(sides[k] * LEV_PAD, LEV_PAD), LEV_PAD), :] = cols.T

    def pick(first, width):
        total = jnp.zeros((CHUNK, width), F32)
        for j in range(4):
            cells = pl.ds(pl.multiple_of(j * CELLS + first, PART), width)
            found = jnp.dot(table[...], picker[:, cells], preferred_element_type=F32)
            code = child[j : j + 1, pl.ds(pl.multiple_of(first, PART), width)]
            group = ((code >> 9) & 1) * N_MEM + (code >> 10)
            for g in range(GROUPS):
                total = total + jnp.where(group == g, found[g * CHUNK : (g + 1) * CHUNK, :], 0.0)
        return (0.25 * total).astype(BF16)

    def far_copy(sub, i):
        return remote(
            coarse_far.at[sub, mem], coarse_far.at[sub, mem], e_send.at[sub, i], e_recv.at[sub, i],
            mem_at(MEM_STEPS[i]), space,
        )

    partner = mem_at((0, 1))

    def rest_copy(i):
        owner = mem if i < 4 else partner
        target = mem_at(((0, 1), (2, 0), (1, 0), (3, 0), (2, 0), (1, 0), (3, 0))[i])
        return remote(coarse_rest.at[owner], coarse_rest.at[owner], c_send.at[i], c_recv.at[i], target, space)

    far = core * (CELLS - HALO)
    near = (1 - core) * (CELLS - HALO)
    for sub in range(2):
        coarse_far[sub, mem] = pick(far + sub * PART, PART)
        for i in range(N_MEM - 1):
            far_copy(sub, i).start()
    coarse_rest[mem, :, 0:HALO] = pick(near, HALO)
    coarse_rest[mem, :, HALO : 2 * HALO] = pick(HALO, HALO)
    coarse_rest[mem, :, 2 * HALO : 3 * HALO] = pick(2 * HALO, HALO)
    for i in range(4):
        rest_copy(i).start()

    two = modes_two[...].astype(BF16)

    def reduce_cells(pair, first, coarse):
        width = coarse.shape[1]
        for i in range(2):
            pert = ens[2 * pair + i, :, pl.ds(pl.multiple_of(first, PART), width)]
            prod[i * LEV_PAD : i * LEV_PAD + LEV, 0:width] = pert * coarse
        value = jnp.dot(two, prod[:, 0:width], preferred_element_type=F32).astype(BF16)
        red[pair * ROWS : (pair + 1) * ROWS, pl.ds(pl.multiple_of(HALO + first, PART), width)] = value

    def halo_copy(n):
        first, place, target, width = (
            (far, (1 - core) * (HALO + CELLS), lax.rem(space + 2 * core + N_SPACE - 1, N_SPACE), PART),
            (far + PART, (1 - core) * (HALO + CELLS) + PART, lax.rem(space + 2 * core + N_SPACE - 1, N_SPACE), PART),
            (near, core * (HALO + CELLS), space + 1 - 2 * core, HALO),
        )[n]
        return remote(
            red.at[:, pl.ds(pl.multiple_of(HALO + first, PART), width)],
            red.at[:, pl.ds(pl.multiple_of(place, PART), width)],
            h_send.at[n], h_recv.at[n], mem, target,
        )

    loads[3].wait()
    for sub in range(2):
        for i in range(N_MEM - 1):
            far_copy(sub, i).wait()
        coarse = coarse_far[sub].reshape(LEV_PAD, PART)[0:LEV]
        for pair in range(PAIRS):
            reduce_cells(pair, far + sub * PART, coarse)
        halo_copy(sub).start()

    rest_copy(0).wait()
    for i in range(4, N_MEM - 1):
        rest_copy(i).start()
    for i in range(1, N_MEM - 1):
        rest_copy(i).wait()
    coarse = coarse_rest[:, :, 0:HALO].reshape(LEV_PAD, HALO)[0:LEV]
    for pair in range(PAIRS):
        reduce_cells(pair, near, coarse)
    halo_copy(2).start()
    for half in range(2):
        coarse = coarse_rest[:, :, (half + 1) * HALO : (half + 2) * HALO].reshape(LEV_PAD, HALO)[0:LEV]
        for pair in range(PAIRS):
            reduce_cells(pair, HALO * (half + 1), coarse)

    loads[4].wait()
    for part in range(MID // PART):
        cells = part * PART
        weights = paired(stencil[:, cells : cells + TILE], stencil[:, cells + TILE : cells + PART])
        window = red[:, HALO + cells : HALO + cells + SPAN]
        mid_out[:, cells : cells + PART] = jnp.dot(window, weights, preferred_element_type=F32)

    for n in range(3):
        halo_copy(n).wait()


def edge_kernel(halo_rows, ext, stencil, mid, out, result, sems):
    mid_copy = pltpu.make_async_copy(mid, out.at[:, pl.ds(HALO, MID)], sems.at[0])
    mid_copy.start()
    copies = [mid_copy]

    col = lax.broadcasted_iota(jnp.int32, (16, HALO), 1)
    low_kept = (col >= HALO - halo_rows[0, 0]).astype(F32).astype(BF16)[0:1]
    high_kept = (col < halo_rows[0, 1]).astype(F32).astype(BF16)[0:1]
    low = ext[:, 0:HALO] * low_kept
    high = ext[:, HALO + CELLS : EXT] * high_kept

    for n, part in enumerate((0, 1, CELLS // PART - 2, CELLS // PART - 1)):
        cells = part * PART
        if part < 2:
            window = jnp.concatenate([low[:, cells:], ext[:, HALO : cells + SPAN]], axis=1)
        else:
            window = jnp.concatenate(
                [ext[:, cells : HALO + CELLS], high[:, 0 : cells + SPAN - HALO - CELLS]], axis=1
            )
        weights = paired(stencil[:, cells : cells + TILE], stencil[:, cells + TILE : cells + PART])
        result[n] = jnp.dot(window, weights, preferred_element_type=F32)
        copy = pltpu.make_async_copy(result.at[n], out.at[:, pl.ds(cells, PART)], sems.at[n + 1])
        copy.start()
        copies.append(copy)
    for copy in copies:
        copy.wait()


def local(ens_pert, vert_modes, loc_stencil, grad_hi, child_map, halo_rows):
    vmem = pl.BlockSpec(memory_space=pltpu.VMEM)
    hbm = pl.BlockSpec(memory_space=pltpu.HBM)
    anywhere = pl.BlockSpec(memory_space=pl.ANY)
    dma = pltpu.SemaphoreType.DMA
    held = [
        pltpu.with_memory_space_constraint(x, pltpu.HBM)
        for x in (grad_hi, child_map, vert_modes.T, ens_pert, loc_stencil)
    ]
    ext, mid = pl.pallas_call(
        reduce_kernel,
        out_shape=(
            jax.ShapeDtypeStruct((ALL_ROWS, EXT), BF16),
            jax.ShapeDtypeStruct((ALL_ROWS, MID), F32),
        ),
        in_specs=[hbm] * 5,
        out_specs=(vmem, vmem),
        scratch_shapes=[
            pltpu.VMEM((LEV, HI), F32),
            pltpu.VMEM((4, CELLS), jnp.int32),
            pltpu.VMEM((MODES, LEV), BF16),
            pltpu.VMEM((2 * PAIRS, LEV, CELLS), BF16),
            pltpu.VMEM((TILE + 2 * HALO, MID), BF16),
            pltpu.VMEM((N_MEM, CHUNK, HI), BF16),
            pltpu.VMEM((N_MEM, CHUNK, HI), BF16),
            pltpu.VMEM((N_SPACE, SEND, LEV_PAD), BF16),
            pltpu.VMEM((N_SPACE, SEND, LEV_PAD), BF16),
            pltpu.VMEM((2 * LEV_PAD, CODES), BF16),
            pltpu.VMEM((CODES, 4 * CELLS), BF16),
            pltpu.VMEM((2, N_MEM, CHUNK, PART), BF16),
            pltpu.VMEM((N_MEM, CHUNK, 3 * HALO), BF16),
            pltpu.VMEM((2 * LEV_PAD, HALO), BF16),
            pltpu.VMEM((ROWS, 2 * LEV_PAD), F32),
            dma((5,)),
            dma((2, N_MEM)),
            dma((2, N_MEM)),
            dma((2, N_SPACE // 2)),
            dma((2, N_SPACE // 2)),
            dma((2, N_MEM)),
            dma((2, N_MEM)),
            dma((N_MEM,)),
            dma((N_MEM,)),
            dma((3,)),
            dma((3,)),
        ],
        compiler_params=pltpu.CompilerParams(
            collective_id=0, has_side_effects=True, vmem_limit_bytes=40 * 2**20
        ),
        name="reduce",
    )(*held)

    out = pl.pallas_call(
        edge_kernel,
        out_shape=jax.ShapeDtypeStruct((ALL_ROWS, CELLS), F32),
        in_specs=[pl.BlockSpec(memory_space=pltpu.SMEM), vmem, vmem, anywhere],
        out_specs=anywhere,
        scratch_shapes=[pltpu.VMEM((4, ALL_ROWS, PART), F32), dma((5,))],
        compiler_params=pltpu.CompilerParams(vmem_limit_bytes=40 * 2**20),
        name="edges",
    )(halo_rows.T, ext, loc_stencil, mid)
    return out.reshape(2 * PAIRS, MODES, CELLS)


def solution(mesh):
    placed = (
        P("mem", None, "space"),
        P(),
        P(None, "space"),
        P(None, ("mem", "space")),
        P(None, "space"),
        P(None, "space"),
    )
    return jax.shard_map(
        local, mesh=mesh, in_specs=placed, out_specs=P("mem", None, "space"), check_vma=False
    )
```

```python
import jax
import jax.numpy as jnp
from jax import lax
from jax.experimental import pallas as pl
from jax.experimental.pallas import tpu as pltpu
from jax.sharding import PartitionSpec as P

MESH = pl.DeviceIdType.MESH
BF16 = jnp.bfloat16
F32 = jnp.float32

TILE = 128
HALO = 512
LEV = 127
LEV_PAD = 128
MODES = 40
CELLS = 2048
EXT = CELLS + 2 * HALO
N_MEM = 8
N_SPACE = 32
CHUNK = LEV_PAD // N_MEM
HI = 1024
SEND = HI // N_SPACE
CODES = 512
GROUPS = N_MEM * HI // CODES
PAIRS = 5
ROWS = 2 * MODES
ALL_ROWS = PAIRS * ROWS
MID = CELLS - 2 * HALO
FAR_SUBS = ((0, 2 * TILE), (2 * TILE, HALO - 2 * TILE))
PART = 2 * TILE
SPAN = PART + 2 * HALO

MEM_STEPS = ((2, 1), (1, 1), (3, 1), (0, 1), (2, 0), (1, 0), (3, 0))
Z_STEPS = (4, 3, 5, 2, 6, 1, 7, 0)
OWN_STEPS = [(z, c) for z in Z_STEPS for c in (1, 0) if z or c]
OTHER_STEPS = [(z, c) for z in Z_STEPS for c in (1, 0)]


def remote(src, dst, send, recv, mem, space):
    return pltpu.make_async_remote_copy(
        src_ref=src,
        dst_ref=dst,
        send_sem=send,
        recv_sem=recv,
        device_id=(mem, space),
        device_id_type=MESH,
    )


def paired(stencil, cells, low, high):
    depth = TILE + 2 * HALO
    even = [stencil[low : min(high, depth), cells : cells + TILE]]
    if high > depth:
        even.append(jnp.zeros((high - depth, TILE), BF16))
    odd = [stencil[max(low - TILE, 0) : high - TILE, cells + TILE : cells + PART]]
    if low < TILE:
        odd.insert(0, jnp.zeros((TILE - low, TILE), BF16))
    return jnp.concatenate([jnp.concatenate(even, axis=0), jnp.concatenate(odd, axis=0)], axis=1)


def own_rows(cells):
    return max(HALO - cells, 0), min(SPAN, HALO + CELLS - cells)


def reduce_kernel(
    grad_hbm, child_hbm, modes_hbm, ens_hbm, stencil_hbm, red, own, stencil,
    grad, child, modes, ens, gb, got_levels, turned, got_cols, table, picker,
    coarse_far, coarse_near, coarse_mid, prod, modes_two,
    in_sem, m_send, m_recv, s_send, s_recv, e_send, e_recv, n_send, n_recv, c_send, c_recv, f_send, f_recv, h_send, h_recv,
):
    mem = lax.axis_index("mem")
    space = lax.axis_index("space")
    y, x_hi = mem // 2, lax.rem(mem, 2)
    x_lo, z, core = space // 16, lax.rem(space // 2, 8), lax.rem(space, 2)

    def mem_at(step):
        return lax.rem(y + step[0], 4) * 2 + lax.rem(x_hi + step[1], 2)

    def space_at(x, step):
        return x * 16 + lax.rem(z + step[0], 8) * 2 + lax.rem(core + step[1], 2)

    loads = [
        pltpu.make_async_copy(src, dst, in_sem.at[i])
        for i, (src, dst) in enumerate(
            (
                (grad_hbm, grad),
                (modes_hbm, modes),
                (child_hbm, child),
                (ens_hbm, ens),
                (stencil_hbm, stencil),
            )
        )
    ]
    loads[0].start()

    barrier = pltpu.get_barrier_semaphore()
    for step in OTHER_STEPS:
        pl.semaphore_signal(barrier, inc=1, device_id=(mem, space_at(1 - x_lo, step)), device_id_type=MESH)
    for step in MEM_STEPS:
        pl.semaphore_signal(barrier, inc=1, device_id=(mem_at(step), space), device_id_type=MESH)
    for step in OWN_STEPS:
        pl.semaphore_signal(barrier, inc=1, device_id=(mem, space_at(x_lo, step)), device_id_type=MESH)

    loads[0].wait()
    for m in range(N_MEM - 1):
        gb[m] = grad[m * CHUNK : (m + 1) * CHUNK, :].astype(BF16)
    last = grad[(N_MEM - 1) * CHUNK : LEV, :]
    gb[N_MEM - 1] = jnp.concatenate([last, jnp.zeros((1, HI), F32)], axis=0).astype(BF16)

    pl.semaphore_wait(barrier, N_MEM - 1 + N_SPACE - 1)

    sides = (x_lo, 1 - x_lo)

    def level_copy(k, i):
        target = mem_at(MEM_STEPS[i])
        cols = pl.ds(pl.multiple_of(sides[k] * CODES, CODES), CODES)
        return remote(
            gb.at[target, :, cols], got_levels.at[mem, :, cols], m_send.at[k, i], m_recv.at[k, i], target, space
        )

    for k in range(2):
        for i in range(N_MEM - 1):
            level_copy(k, i).start()
    for load in loads[1:]:
        load.start()

    got_levels[mem] = gb[mem]

    loads[1].wait()
    modes_two[...] = jnp.zeros_like(modes_two)
    wide = modes[...].astype(F32)
    modes_two[0:MODES, 0:LEV] = wide
    modes_two[MODES:ROWS, LEV_PAD : LEV_PAD + LEV] = wide
    prod[...] = jnp.zeros_like(prod)

    def column_copy(k, i):
        target = space_at(sides[k], (OWN_STEPS, OTHER_STEPS)[k][i])
        return remote(turned.at[target], got_cols.at[space], s_send.at[k, i], s_recv.at[k, i], mem, target)

    counts = (len(OWN_STEPS), len(OTHER_STEPS))
    for k in range(2):
        for i in range(N_MEM - 1):
            level_copy(k, i).wait()
        for q in range(CODES // 128):
            first = pl.multiple_of(sides[k] * CODES + q * 128, 128)
            part = got_levels[:, :, pl.ds(first, 128)].reshape(LEV_PAD, 128)
            turned[pl.ds(sides[k] * 16 + q * 4, 4)] = part.T.reshape(4, SEND, LEV_PAD)
        for i in range(counts[k]):
            column_copy(k, i).start()

    got_cols[space] = turned[space]
    loads[2].wait()

    @pl.loop(0, 4 * CELLS // 256)
    def _(t):
        j = t // (CELLS // 256)
        first = pl.multiple_of(lax.rem(t, CELLS // 256) * 256, 256)
        low = child[pl.ds(j, 1), pl.ds(first, 256)] & (CODES - 1)
        hot = lax.broadcasted_iota(jnp.int32, (CODES, 256), 0) == low
        picker[:, pl.ds(pl.multiple_of(t * 256, 256), 256)] = hot.astype(F32).astype(BF16)

    for k in range(2):
        for i in range(counts[k]):
            column_copy(k, i).wait()
        cols = got_cols[pl.ds(sides[k] * 16, 16)].reshape(CODES, LEV_PAD)
        table[pl.ds(pl.multiple_of(sides[k] * LEV_PAD, LEV_PAD), LEV_PAD), :] = cols.T

    def pick(first, width):
        total = jnp.zeros((CHUNK, width), F32)
        for j in range(4):
            cells = pl.ds(pl.multiple_of(j * CELLS + first, TILE), width)
            found = jnp.dot(table[...], picker[:, cells], preferred_element_type=F32)
            code = child[j : j + 1, pl.ds(pl.multiple_of(first, TILE), width)]
            group = ((code >> 9) & 1) * N_MEM + (code >> 10)
            for g in range(GROUPS):
                total = total + jnp.where(group == g, found[g * CHUNK : (g + 1) * CHUNK, :], 0.0)
        return (0.25 * total).astype(BF16)

    def far_copy(sub, i):
        cols = pl.ds(*FAR_SUBS[sub])
        return remote(
            coarse_far.at[mem, :, cols], coarse_far.at[mem, :, cols], e_send.at[sub, i], e_recv.at[sub, i],
            mem_at(MEM_STEPS[i]), space,
        )

    def near_copy(i):
        return remote(
            coarse_near.at[mem], coarse_near.at[mem], n_send.at[i], n_recv.at[i], mem_at(MEM_STEPS[i]), space
        )

    partner = mem_at((0, 1))

    def mid_copy(half, i):
        owner = mem if i < 4 else partner
        target = mem_at(((0, 1), (2, 0), (1, 0), (3, 0), (2, 0), (1, 0), (3, 0))[i])
        return remote(
            coarse_mid.at[half, owner], coarse_mid.at[half, owner], c_send.at[half, i], c_recv.at[half, i], target, space
        )

    far = core * (CELLS - HALO)
    near = (1 - core) * (CELLS - HALO)
    for sub, (cells, width) in enumerate(FAR_SUBS):
        coarse_far[mem, :, cells : cells + width] = pick(far + cells, width)
        for i in range(N_MEM - 1):
            far_copy(sub, i).start()
    for half in range(2):
        coarse_mid[half, mem] = pick(HALO * (half + 1), HALO)
        for i in range(4):
            mid_copy(half, i).start()
    coarse_near[mem] = pick(near, HALO)
    for i in range(N_MEM - 1):
        near_copy(i).start()

    two = modes_two[...].astype(BF16)

    def reduce_cells(pair, first, coarse):
        width = coarse.shape[1]
        for i in range(2):
            pert = ens[2 * pair + i, :, pl.ds(pl.multiple_of(first, TILE), width)]
            prod[i * LEV_PAD : i * LEV_PAD + LEV, 0:width] = pert * coarse
        value = jnp.dot(two, prod[:, 0:width], preferred_element_type=F32).astype(BF16)
        red[pair * ROWS : (pair + 1) * ROWS, pl.ds(pl.multiple_of(HALO + first, TILE), width)] = value

    far_target = lax.rem(space + 2 * core + N_SPACE - 1, N_SPACE)
    far_place = (1 - core) * (HALO + CELLS)

    def far_halo(sub):
        cells, width = FAR_SUBS[sub]
        return remote(
            red.at[:, pl.ds(pl.multiple_of(HALO + far + cells, TILE), width)],
            red.at[:, pl.ds(pl.multiple_of(far_place + cells, TILE), width)],
            f_send.at[sub], f_recv.at[sub], mem, far_target,
        )

    def near_halo(pair):
        rows = pl.ds(pair * ROWS, ROWS)
        return remote(
            red.at[rows, pl.ds(pl.multiple_of(HALO + near, HALO), HALO)],
            red.at[rows, pl.ds(pl.multiple_of(core * (HALO + CELLS), HALO), HALO)],
            h_send.at[pair], h_recv.at[pair], mem, space + 1 - 2 * core,
        )

    loads[3].wait()
    for sub, (cells, width) in enumerate(FAR_SUBS):
        for i in range(N_MEM - 1):
            far_copy(sub, i).wait()
        coarse = coarse_far[:, :, cells : cells + width].reshape(LEV_PAD, width)[0:LEV]
        for pair in range(PAIRS):
            reduce_cells(pair, far + cells, coarse)
        far_halo(sub).start()

    for half in range(2):
        mid_copy(half, 0).wait()
        for i in range(4, N_MEM - 1):
            mid_copy(half, i).start()

    for i in range(N_MEM - 1):
        near_copy(i).wait()
    coarse = coarse_near[...].reshape(LEV_PAD, HALO)[0:LEV]
    for pair in range(PAIRS):
        reduce_cells(pair, near, coarse)
        near_halo(pair).start()

    loads[4].wait()
    done = 0
    for half in range(2):
        for i in range(1, N_MEM - 1):
            mid_copy(half, i).wait()
        coarse = coarse_mid[half].reshape(LEV_PAD, HALO)[0:LEV]
        for pair in range(PAIRS):
            reduce_cells(pair, HALO * (half + 1), coarse)
        for part in range(done, (2, CELLS // PART)[half]):
            cells = part * PART
            low, high = own_rows(cells)
            own[:, cells : cells + PART] = jnp.dot(
                red[:, cells + low : cells + high], paired(stencil, cells, low, high), preferred_element_type=F32
            )
        done = 2

    for pair in range(PAIRS):
        near_halo(pair).wait()
    for sub in range(2):
        far_halo(sub).wait()


def edge_kernel(halo_rows, ext, own, stencil, out, result, sems):
    mid_copy = pltpu.make_async_copy(own.at[:, pl.ds(HALO, MID)], out.at[:, pl.ds(HALO, MID)], sems.at[0])
    mid_copy.start()
    copies = [mid_copy]

    col = lax.broadcasted_iota(jnp.int32, (16, HALO), 1)
    low_kept = (col >= HALO - halo_rows[0, 0]).astype(F32).astype(BF16)[0:1]
    high_kept = (col < halo_rows[0, 1]).astype(F32).astype(BF16)[0:1]

    for n, part in enumerate((0, 1, CELLS // PART - 2, CELLS // PART - 1)):
        cells = part * PART
        low, high = own_rows(cells)
        if part < 2:
            low, high = 0, low
            kept = low_kept[:, cells:]
        else:
            low, high = high, SPAN
            kept = high_kept[:, 0 : high - low]
        window = ext[:, cells + low : cells + high] * kept
        result[n] = own[:, cells : cells + PART] + jnp.dot(
            window, paired(stencil, cells, low, high), preferred_element_type=F32
        )
        copy = pltpu.make_async_copy(result.at[n], out.at[:, pl.ds(cells, PART)], sems.at[n + 1])
        copy.start()
        copies.append(copy)
    for copy in copies:
        copy.wait()


def local(ens_pert, vert_modes, loc_stencil, grad_hi, child_map, halo_rows):
    vmem = pl.BlockSpec(memory_space=pltpu.VMEM)
    hbm = pl.BlockSpec(memory_space=pltpu.HBM)
    anywhere = pl.BlockSpec(memory_space=pl.ANY)
    dma = pltpu.SemaphoreType.DMA
    held = [
        pltpu.with_memory_space_constraint(x, pltpu.HBM)
        for x in (grad_hi, child_map, vert_modes.T, ens_pert, loc_stencil)
    ]
    ext, own, stencil = pl.pallas_call(
        reduce_kernel,
        out_shape=(
            jax.ShapeDtypeStruct((ALL_ROWS, EXT), BF16),
            jax.ShapeDtypeStruct((ALL_ROWS, CELLS), F32),
            jax.ShapeDtypeStruct((TILE + 2 * HALO, CELLS), BF16),
        ),
        in_specs=[hbm] * 5,
        out_specs=(vmem, vmem, vmem),
        scratch_shapes=[
            pltpu.VMEM((LEV, HI), F32),
            pltpu.VMEM((4, CELLS), jnp.int32),
            pltpu.VMEM((MODES, LEV), BF16),
            pltpu.VMEM((2 * PAIRS, LEV, CELLS), BF16),
            pltpu.VMEM((N_MEM, CHUNK, HI), BF16),
            pltpu.VMEM((N_MEM, CHUNK, HI), BF16),
            pltpu.VMEM((N_SPACE, SEND, LEV_PAD), BF16),
            pltpu.VMEM((N_SPACE, SEND, LEV_PAD), BF16),
            pltpu.VMEM((2 * LEV_PAD, CODES), BF16),
            pltpu.VMEM((CODES, 4 * CELLS), BF16),
            pltpu.VMEM((N_MEM, CHUNK, HALO), BF16),
            pltpu.VMEM((N_MEM, CHUNK, HALO), BF16),
            pltpu.VMEM((2, N_MEM, CHUNK, HALO), BF16),
            pltpu.VMEM((2 * LEV_PAD, HALO), BF16),
            pltpu.VMEM((ROWS, 2 * LEV_PAD), F32),
            dma((5,)),
            dma((2, N_MEM)),
            dma((2, N_MEM)),
            dma((2, N_SPACE // 2)),
            dma((2, N_SPACE // 2)),
            dma((2, N_MEM)),
            dma((2, N_MEM)),
            dma((N_MEM,)),
            dma((N_MEM,)),
            dma((2, N_MEM)),
            dma((2, N_MEM)),
            dma((2,)),
            dma((2,)),
            dma((PAIRS,)),
            dma((PAIRS,)),
        ],
        compiler_params=pltpu.CompilerParams(
            collective_id=0, has_side_effects=True, vmem_limit_bytes=40 * 2**20
        ),
        name="reduce",
    )(*held)

    out = pl.pallas_call(
        edge_kernel,
        out_shape=jax.ShapeDtypeStruct((ALL_ROWS, CELLS), F32),
        in_specs=[pl.BlockSpec(memory_space=pltpu.SMEM), vmem, vmem, vmem],
        out_specs=anywhere,
        scratch_shapes=[pltpu.VMEM((4, ALL_ROWS, PART), F32), dma((5,))],
        compiler_params=pltpu.CompilerParams(vmem_limit_bytes=40 * 2**20),
        name="edges",
    )(halo_rows.T, ext, own, stencil)
    return out.reshape(2 * PAIRS, MODES, CELLS)


def solution(mesh):
    placed = (
        P("mem", None, "space"),
        P(),
        P(None, "space"),
        P(None, ("mem", "space")),
        P(None, "space"),
        P(None, "space"),
    )
    return jax.shard_map(
        local, mesh=mesh, in_specs=placed, out_specs=P("mem", None, "space"), check_vma=False
    )
```

```python
import jax
import jax.numpy as jnp
from jax import lax
from jax.experimental import pallas as pl
from jax.experimental.pallas import tpu as pltpu
from jax.sharding import PartitionSpec as P

MESH = pl.DeviceIdType.MESH
BF16 = jnp.bfloat16
F32 = jnp.float32

TILE = 128
HALO = 512
LEV = 127
LEV_PAD = 128
MODES = 40
CELLS = 2048
EXT = CELLS + 2 * HALO
N_MEM = 8
N_SPACE = 32
CHUNK = LEV_PAD // N_MEM
HI = 1024
SEND = HI // N_SPACE
CODES = 512
GROUPS = N_MEM * HI // CODES
PAIRS = 5
ROWS = 2 * MODES
ALL_ROWS = PAIRS * ROWS
MID = CELLS - 2 * HALO
FAR_SUBS = ((0, 2 * TILE), (2 * TILE, HALO - 2 * TILE))
PART = 2 * TILE
SPAN = PART + 2 * HALO

MEM_STEPS = ((2, 1), (1, 1), (3, 1), (0, 1), (2, 0), (1, 0), (3, 0))
Z_STEPS = (4, 3, 5, 2, 6, 1, 7, 0)
OWN_STEPS = [(z, c) for z in Z_STEPS for c in (1, 0) if z or c]
OTHER_STEPS = [(z, c) for z in Z_STEPS for c in (1, 0)]


def remote(src, dst, send, recv, mem, space):
    return pltpu.make_async_remote_copy(
        src_ref=src,
        dst_ref=dst,
        send_sem=send,
        recv_sem=recv,
        device_id=(mem, space),
        device_id_type=MESH,
    )


def paired(stencil, cells, low, high):
    depth = TILE + 2 * HALO
    even = [stencil[low : min(high, depth), cells : cells + TILE]]
    if high > depth:
        even.append(jnp.zeros((high - depth, TILE), BF16))
    odd = [stencil[max(low - TILE, 0) : high - TILE, cells + TILE : cells + PART]]
    if low < TILE:
        odd.insert(0, jnp.zeros((TILE - low, TILE), BF16))
    return jnp.concatenate([jnp.concatenate(even, axis=0), jnp.concatenate(odd, axis=0)], axis=1)


def own_rows(cells):
    return max(HALO - cells, 0), min(SPAN, HALO + CELLS - cells)


def reduce_kernel(
    grad_hbm, child_hbm, modes_hbm, ens_hbm, stencil_hbm, red, own, stencil,
    grad, child, modes, ens, gb, got_levels, turned, got_cols, table, picker,
    coarse_far, coarse_near, coarse_mid, prod, modes_two,
    in_sem, m_send, m_recv, s_send, s_recv, e_send, e_recv, n_send, n_recv, c_send, c_recv, f_send, f_recv, h_send, h_recv,
):
    mem = lax.axis_index("mem")
    space = lax.axis_index("space")
    y, x_hi = mem // 2, lax.rem(mem, 2)
    x_lo, z, core = space // 16, lax.rem(space // 2, 8), lax.rem(space, 2)

    def mem_at(step):
        return lax.rem(y + step[0], 4) * 2 + lax.rem(x_hi + step[1], 2)

    def space_at(x, step):
        return x * 16 + lax.rem(z + step[0], 8) * 2 + lax.rem(core + step[1], 2)

    loads = [
        pltpu.make_async_copy(src, dst, in_sem.at[i])
        for i, (src, dst) in enumerate(
            (
                (grad_hbm, grad),
                (modes_hbm, modes),
                (child_hbm, child),
                (ens_hbm, ens),
                (stencil_hbm, stencil),
            )
        )
    ]
    loads[0].start()

    barrier = pltpu.get_barrier_semaphore()
    for step in OTHER_STEPS:
        pl.semaphore_signal(barrier, inc=1, device_id=(mem, space_at(1 - x_lo, step)), device_id_type=MESH)
    for step in MEM_STEPS:
        pl.semaphore_signal(barrier, inc=1, device_id=(mem_at(step), space), device_id_type=MESH)
    for step in OWN_STEPS:
        pl.semaphore_signal(barrier, inc=1, device_id=(mem, space_at(x_lo, step)), device_id_type=MESH)

    loads[0].wait()
    for m in range(N_MEM - 1):
        gb[m] = grad[m * CHUNK : (m + 1) * CHUNK, :].astype(BF16)
    last = grad[(N_MEM - 1) * CHUNK : LEV, :]
    gb[N_MEM - 1] = jnp.concatenate([last, jnp.zeros((1, HI), F32)], axis=0).astype(BF16)

    pl.semaphore_wait(barrier, N_MEM - 1 + N_SPACE - 1)

    sides = (1 - x_lo, x_lo)

    def level_copy(k, i):
        target = mem_at(MEM_STEPS[i])
        cols = pl.ds(pl.multiple_of(sides[k] * CODES, CODES), CODES)
        return remote(
            gb.at[target, :, cols], got_levels.at[mem, :, cols], m_send.at[k, i], m_recv.at[k, i], target, space
        )

    for k in range(2):
        for i in range(N_MEM - 1):
            level_copy(k, i).start()
    for load in loads[1:]:
        load.start()

    got_levels[mem] = gb[mem]

    loads[1].wait()
    modes_two[...] = jnp.zeros_like(modes_two)
    wide = modes[...].astype(F32)
    modes_two[0:MODES, 0:LEV] = wide
    modes_two[MODES:ROWS, LEV_PAD : LEV_PAD + LEV] = wide
    prod[...] = jnp.zeros_like(prod)

    def column_copy(k, i):
        target = space_at(sides[k], (OTHER_STEPS, OWN_STEPS)[k][i])
        return remote(turned.at[target], got_cols.at[space], s_send.at[k, i], s_recv.at[k, i], mem, target)

    counts = (len(OTHER_STEPS), len(OWN_STEPS))
    for k in range(2):
        for i in range(N_MEM - 1):
            level_copy(k, i).wait()
        for q in range(CODES // 128):
            first = pl.multiple_of(sides[k] * CODES + q * 128, 128)
            part = got_levels[:, :, pl.ds(first, 128)].reshape(LEV_PAD, 128)
            turned[pl.ds(sides[k] * 16 + q * 4, 4)] = part.T.reshape(4, SEND, LEV_PAD)
        for i in range(counts[k]):
            column_copy(k, i).start()

    got_cols[space] = turned[space]
    loads[2].wait()

    @pl.loop(0, 4 * CELLS // 256)
    def _(t):
        j = t // (CELLS // 256)
        first = pl.multiple_of(lax.rem(t, CELLS // 256) * 256, 256)
        low = child[pl.ds(j, 1), pl.ds(first, 256)] & (CODES - 1)
        hot = lax.broadcasted_iota(jnp.int32, (CODES, 256), 0) == low
        picker[:, pl.ds(pl.multiple_of(t * 256, 256), 256)] = hot.astype(F32).astype(BF16)

    for k in range(2):
        for i in range(counts[k]):
            column_copy(k, i).wait()
        cols = got_cols[pl.ds(sides[k] * 16, 16)].reshape(CODES, LEV_PAD)
        table[pl.ds(pl.multiple_of(sides[k] * LEV_PAD, LEV_PAD), LEV_PAD), :] = cols.T

    def pick(first, width):
        total = jnp.zeros((CHUNK, width), F32)
        for j in range(4):
            cells = pl.ds(pl.multiple_of(j * CELLS + first, TILE), width)
            found = jnp.dot(table[...], picker[:, cells], preferred_element_type=F32)
            code = child[j : j + 1, pl.ds(pl.multiple_of(first, TILE), width)]
            group = ((code >> 9) & 1) * N_MEM + (code >> 10)
            for g in range(GROUPS):
                total = total + jnp.where(group == g, found[g * CHUNK : (g + 1) * CHUNK, :], 0.0)
        return (0.25 * total).astype(BF16)

    def far_copy(sub, i):
        cols = pl.ds(*FAR_SUBS[sub])
        return remote(
            coarse_far.at[mem, :, cols], coarse_far.at[mem, :, cols], e_send.at[sub, i], e_recv.at[sub, i],
            mem_at(MEM_STEPS[i]), space,
        )

    def near_copy(i):
        return remote(
            coarse_near.at[mem], coarse_near.at[mem], n_send.at[i], n_recv.at[i], mem_at(MEM_STEPS[i]), space
        )

    partner = mem_at((0, 1))

    def mid_copy(half, i):
        owner = mem if i < 4 else partner
        target = mem_at(((0, 1), (2, 0), (1, 0), (3, 0), (2, 0), (1, 0), (3, 0))[i])
        return remote(
            coarse_mid.at[half, owner], coarse_mid.at[half, owner], c_send.at[half, i], c_recv.at[half, i], target, space
        )

    far = core * (CELLS - HALO)
    near = (1 - core) * (CELLS - HALO)
    for sub, (cells, width) in enumerate(FAR_SUBS):
        coarse_far[mem, :, cells : cells + width] = pick(far + cells, width)
        for i in range(N_MEM - 1):
            far_copy(sub, i).start()
    for half in range(2):
        coarse_mid[half, mem] = pick(HALO * (half + 1), HALO)
        for i in range(4):
            mid_copy(half, i).start()
    coarse_near[mem] = pick(near, HALO)
    for i in range(N_MEM - 1):
        near_copy(i).start()

    two = modes_two[...].astype(BF16)

    def reduce_cells(pair, first, coarse):
        width = coarse.shape[1]
        for i in range(2):
            pert = ens[2 * pair + i, :, pl.ds(pl.multiple_of(first, TILE), width)]
            prod[pair, i * LEV_PAD : i * LEV_PAD + LEV, 0:width] = pert * coarse
        value = jnp.dot(two, prod[pair, :, 0:width], preferred_element_type=F32).astype(BF16)
        red[pair * ROWS : (pair + 1) * ROWS, pl.ds(pl.multiple_of(HALO + first, TILE), width)] = value

    far_target = lax.rem(space + 2 * core + N_SPACE - 1, N_SPACE)
    far_place = (1 - core) * (HALO + CELLS)

    def far_halo(sub):
        cells, width = FAR_SUBS[sub]
        return remote(
            red.at[:, pl.ds(pl.multiple_of(HALO + far + cells, TILE), width)],
            red.at[:, pl.ds(pl.multiple_of(far_place + cells, TILE), width)],
            f_send.at[sub], f_recv.at[sub], mem, far_target,
        )

    def near_halo(pair):
        rows = pl.ds(pair * ROWS, ROWS)
        return remote(
            red.at[rows, pl.ds(pl.multiple_of(HALO + near, HALO), HALO)],
            red.at[rows, pl.ds(pl.multiple_of(core * (HALO + CELLS), HALO), HALO)],
            h_send.at[pair], h_recv.at[pair], mem, space + 1 - 2 * core,
        )

    loads[3].wait()
    for sub, (cells, width) in enumerate(FAR_SUBS):
        for i in range(N_MEM - 1):
            far_copy(sub, i).wait()
        coarse = coarse_far[:, :, cells : cells + width].reshape(LEV_PAD, width)[0:LEV]
        for pair in range(PAIRS):
            reduce_cells(pair, far + cells, coarse)
        far_halo(sub).start()

    for half in range(2):
        mid_copy(half, 0).wait()
        for i in range(4, N_MEM - 1):
            mid_copy(half, i).start()

    for i in range(N_MEM - 1):
        near_copy(i).wait()
    coarse = coarse_near[...].reshape(LEV_PAD, HALO)[0:LEV]
    for pair in range(PAIRS):
        reduce_cells(pair, near, coarse)
        near_halo(pair).start()

    loads[4].wait()
    done = 0
    for half in range(2):
        for i in range(1, N_MEM - 1):
            mid_copy(half, i).wait()
        coarse = coarse_mid[half].reshape(LEV_PAD, HALO)[0:LEV]
        for pair in range(PAIRS):
            reduce_cells(pair, HALO * (half + 1), coarse)
        for part in range(done, (2, CELLS // PART)[half]):
            cells = part * PART
            low, high = own_rows(cells)
            own[:, cells : cells + PART] = jnp.dot(
                red[:, cells + low : cells + high], paired(stencil, cells, low, high), preferred_element_type=F32
            )
        done = 2

    for pair in range(PAIRS):
        near_halo(pair).wait()
    for sub in range(2):
        far_halo(sub).wait()


def edge_kernel(halo_rows, ext, own, stencil, out, result, sems):
    mid_copy = pltpu.make_async_copy(own.at[:, pl.ds(HALO, MID)], out.at[:, pl.ds(HALO, MID)], sems.at[0])
    mid_copy.start()
    copies = [mid_copy]

    col = lax.broadcasted_iota(jnp.int32, (16, HALO), 1)
    low_kept = (col >= HALO - halo_rows[0, 0]).astype(F32).astype(BF16)[0:1]
    high_kept = (col < halo_rows[0, 1]).astype(F32).astype(BF16)[0:1]

    for n, part in enumerate((0, 1, CELLS // PART - 2, CELLS // PART - 1)):
        cells = part * PART
        low, high = own_rows(cells)
        if part < 2:
            low, high = 0, low
            kept = low_kept[:, cells:]
        else:
            low, high = high, SPAN
            kept = high_kept[:, 0 : high - low]
        window = ext[:, cells + low : cells + high] * kept
        result[n] = own[:, cells : cells + PART] + jnp.dot(
            window, paired(stencil, cells, low, high), preferred_element_type=F32
        )
        copy = pltpu.make_async_copy(result.at[n], out.at[:, pl.ds(cells, PART)], sems.at[n + 1])
        copy.start()
        copies.append(copy)
    for copy in copies:
        copy.wait()


def local(ens_pert, vert_modes, loc_stencil, grad_hi, child_map, halo_rows):
    vmem = pl.BlockSpec(memory_space=pltpu.VMEM)
    hbm = pl.BlockSpec(memory_space=pltpu.HBM)
    anywhere = pl.BlockSpec(memory_space=pl.ANY)
    dma = pltpu.SemaphoreType.DMA
    held = [
        pltpu.with_memory_space_constraint(x, pltpu.HBM)
        for x in (grad_hi, child_map, vert_modes.T, ens_pert, loc_stencil)
    ]
    ext, own, stencil = pl.pallas_call(
        reduce_kernel,
        out_shape=(
            jax.ShapeDtypeStruct((ALL_ROWS, EXT), BF16),
            jax.ShapeDtypeStruct((ALL_ROWS, CELLS), F32),
            jax.ShapeDtypeStruct((TILE + 2 * HALO, CELLS), BF16),
        ),
        in_specs=[hbm] * 5,
        out_specs=(vmem, vmem, vmem),
        scratch_shapes=[
            pltpu.VMEM((LEV, HI), F32),
            pltpu.VMEM((4, CELLS), jnp.int32),
            pltpu.VMEM((MODES, LEV), BF16),
            pltpu.VMEM((2 * PAIRS, LEV, CELLS), BF16),
            pltpu.VMEM((N_MEM, CHUNK, HI), BF16),
            pltpu.VMEM((N_MEM, CHUNK, HI), BF16),
            pltpu.VMEM((N_SPACE, SEND, LEV_PAD), BF16),
            pltpu.VMEM((N_SPACE, SEND, LEV_PAD), BF16),
            pltpu.VMEM((2 * LEV_PAD, CODES), BF16),
            pltpu.VMEM((CODES, 4 * CELLS), BF16),
            pltpu.VMEM((N_MEM, CHUNK, HALO), BF16),
            pltpu.VMEM((N_MEM, CHUNK, HALO), BF16),
            pltpu.VMEM((2, N_MEM, CHUNK, HALO), BF16),
            pltpu.VMEM((PAIRS, 2 * LEV_PAD, HALO), BF16),
            pltpu.VMEM((ROWS, 2 * LEV_PAD), F32),
            dma((5,)),
            dma((2, N_MEM)),
            dma((2, N_MEM)),
            dma((2, N_SPACE // 2)),
            dma((2, N_SPACE // 2)),
            dma((2, N_MEM)),
            dma((2, N_MEM)),
            dma((N_MEM,)),
            dma((N_MEM,)),
            dma((2, N_MEM)),
            dma((2, N_MEM)),
            dma((2,)),
            dma((2,)),
            dma((PAIRS,)),
            dma((PAIRS,)),
        ],
        compiler_params=pltpu.CompilerParams(
            collective_id=0, has_side_effects=True, vmem_limit_bytes=40 * 2**20
        ),
        name="reduce",
    )(*held)

    out = pl.pallas_call(
        edge_kernel,
        out_shape=jax.ShapeDtypeStruct((ALL_ROWS, CELLS), F32),
        in_specs=[pl.BlockSpec(memory_space=pltpu.SMEM), vmem, vmem, vmem],
        out_specs=anywhere,
        scratch_shapes=[pltpu.VMEM((4, ALL_ROWS, PART), F32), dma((5,))],
        compiler_params=pltpu.CompilerParams(vmem_limit_bytes=40 * 2**20),
        name="edges",
    )(halo_rows.T, ext, own, stencil)
    return out.reshape(2 * PAIRS, MODES, CELLS)


def solution(mesh):
    placed = (
        P("mem", None, "space"),
        P(),
        P(None, "space"),
        P(None, ("mem", "space")),
        P(None, "space"),
        P(None, "space"),
    )
    return jax.shard_map(
        local, mesh=mesh, in_specs=placed, out_specs=P("mem", None, "space"), check_vma=False
    )
```

```python
import jax
import jax.numpy as jnp
from jax import lax
from jax.experimental import pallas as pl
from jax.experimental.pallas import tpu as pltpu
from jax.sharding import PartitionSpec as P

MESH = pl.DeviceIdType.MESH
BF16 = jnp.bfloat16
F32 = jnp.float32

TILE = 128
HALO = 512
LEV = 127
LEV_PAD = 128
MODES = 40
CELLS = 2048
EXT = CELLS + 2 * HALO
N_MEM = 8
N_SPACE = 32
CHUNK = LEV_PAD // N_MEM
HI = 1024
SEND = HI // N_SPACE
CODES = 512
GROUPS = N_MEM * HI // CODES
PAIRS = 5
ROWS = 2 * MODES
ALL_ROWS = PAIRS * ROWS
MID = CELLS - 2 * HALO
FAR_SUBS = ((0, 2 * TILE), (2 * TILE, HALO - 2 * TILE))
PART = 2 * TILE
SPAN = PART + 2 * HALO

MEM_STEPS = ((2, 1), (1, 1), (3, 1), (0, 1), (2, 0), (1, 0), (3, 0))
Z_STEPS = (4, 3, 5, 2, 6, 1, 7, 0)
OWN_STEPS = [(z, c) for z in Z_STEPS for c in (1, 0) if z or c]
OTHER_STEPS = [(z, c) for z in Z_STEPS for c in (1, 0)]


def remote(src, dst, send, recv, mem, space):
    return pltpu.make_async_remote_copy(
        src_ref=src,
        dst_ref=dst,
        send_sem=send,
        recv_sem=recv,
        device_id=(mem, space),
        device_id_type=MESH,
    )


def paired(stencil, cells, low, high):
    depth = TILE + 2 * HALO
    even = [stencil[low : min(high, depth), cells : cells + TILE]]
    if high > depth:
        even.append(jnp.zeros((high - depth, TILE), BF16))
    odd = [stencil[max(low - TILE, 0) : high - TILE, cells + TILE : cells + PART]]
    if low < TILE:
        odd.insert(0, jnp.zeros((TILE - low, TILE), BF16))
    return jnp.concatenate([jnp.concatenate(even, axis=0), jnp.concatenate(odd, axis=0)], axis=1)


def own_rows(cells):
    return max(HALO - cells, 0), min(SPAN, HALO + CELLS - cells)


def reduce_kernel(
    grad_hbm, child_hbm, modes_hbm, ens_hbm, stencil_hbm, red, own, stencil,
    grad, child, modes, ens, gb, got_levels, turned, got_cols, table, picker,
    coarse_far, coarse_near, coarse_mid, prod, modes_two,
    in_sem, m_send, m_recv, s_send, s_recv, e_send, e_recv, n_send, n_recv, c_send, c_recv, f_send, f_recv, h_send, h_recv,
):
    mem = lax.axis_index("mem")
    space = lax.axis_index("space")
    y, x_hi = mem // 2, lax.rem(mem, 2)
    x_lo, z, core = space // 16, lax.rem(space // 2, 8), lax.rem(space, 2)

    def mem_at(step):
        return lax.rem(y + step[0], 4) * 2 + lax.rem(x_hi + step[1], 2)

    def space_at(x, step):
        return x * 16 + lax.rem(z + step[0], 8) * 2 + lax.rem(core + step[1], 2)

    loads = [
        pltpu.make_async_copy(src, dst, in_sem.at[i])
        for i, (src, dst) in enumerate(
            (
                (grad_hbm, grad),
                (modes_hbm, modes),
                (child_hbm, child),
                (ens_hbm, ens),
                (stencil_hbm, stencil),
            )
        )
    ]
    loads[0].start()

    barrier = pltpu.get_barrier_semaphore()
    for step in OTHER_STEPS:
        pl.semaphore_signal(barrier, inc=1, device_id=(mem, space_at(1 - x_lo, step)), device_id_type=MESH)
    for step in MEM_STEPS:
        pl.semaphore_signal(barrier, inc=1, device_id=(mem_at(step), space), device_id_type=MESH)
    for step in OWN_STEPS:
        pl.semaphore_signal(barrier, inc=1, device_id=(mem, space_at(x_lo, step)), device_id_type=MESH)

    loads[0].wait()
    for m in range(N_MEM - 1):
        gb[m] = grad[m * CHUNK : (m + 1) * CHUNK, :].astype(BF16)
    last = grad[(N_MEM - 1) * CHUNK : LEV, :]
    gb[N_MEM - 1] = jnp.concatenate([last, jnp.zeros((1, HI), F32)], axis=0).astype(BF16)

    pl.semaphore_wait(barrier, N_MEM - 1 + N_SPACE - 1)

    sides = (1 - x_lo, x_lo)

    def level_copy(k, i):
        target = mem_at(MEM_STEPS[i])
        cols = pl.ds(pl.multiple_of(sides[k] * CODES, CODES), CODES)
        return remote(
            gb.at[target, :, cols], got_levels.at[mem, :, cols], m_send.at[k, i], m_recv.at[k, i], target, space
        )

    for k in range(2):
        for i in range(N_MEM - 1):
            level_copy(k, i).start()
    for load in loads[1:]:
        load.start()

    got_levels[mem] = gb[mem]

    loads[1].wait()
    modes_two[...] = jnp.zeros_like(modes_two)
    wide = modes[...].astype(F32)
    modes_two[0:MODES, 0:LEV] = wide
    modes_two[MODES:ROWS, LEV_PAD : LEV_PAD + LEV] = wide
    prod[...] = jnp.zeros_like(prod)

    def column_copy(k, i):
        target = space_at(sides[k], (OTHER_STEPS, OWN_STEPS)[k][i])
        return remote(turned.at[target], got_cols.at[space], s_send.at[k, i], s_recv.at[k, i], mem, target)

    counts = (len(OTHER_STEPS), len(OWN_STEPS))
    for k in range(2):
        for i in range(N_MEM - 1):
            level_copy(k, i).wait_recv()
        for q in range(CODES // 128):
            first = pl.multiple_of(sides[k] * CODES + q * 128, 128)
            part = got_levels[:, :, pl.ds(first, 128)].reshape(LEV_PAD, 128)
            turned[pl.ds(sides[k] * 16 + q * 4, 4)] = part.T.reshape(4, SEND, LEV_PAD)
        for i in range(counts[k]):
            column_copy(k, i).start()

    got_cols[space] = turned[space]
    loads[2].wait()

    @pl.loop(0, 4 * CELLS // 256)
    def _(t):
        j = t // (CELLS // 256)
        first = pl.multiple_of(lax.rem(t, CELLS // 256) * 256, 256)
        low = child[pl.ds(j, 1), pl.ds(first, 256)] & (CODES - 1)
        hot = lax.broadcasted_iota(jnp.int32, (CODES, 256), 0) == low
        picker[:, pl.ds(pl.multiple_of(t * 256, 256), 256)] = hot.astype(F32).astype(BF16)

    for k in range(2):
        for i in range(counts[k]):
            column_copy(k, i).wait_recv()
        cols = got_cols[pl.ds(sides[k] * 16, 16)].reshape(CODES, LEV_PAD)
        table[pl.ds(pl.multiple_of(sides[k] * LEV_PAD, LEV_PAD), LEV_PAD), :] = cols.T

    def pick(first, width):
        total = jnp.zeros((CHUNK, width), F32)
        for j in range(4):
            cells = pl.ds(pl.multiple_of(j * CELLS + first, TILE), width)
            found = jnp.dot(table[...], picker[:, cells], preferred_element_type=F32)
            code = child[j : j + 1, pl.ds(pl.multiple_of(first, TILE), width)]
            group = ((code >> 9) & 1) * N_MEM + (code >> 10)
            for g in range(GROUPS):
                total = total + jnp.where(group == g, found[g * CHUNK : (g + 1) * CHUNK, :], 0.0)
        return (0.25 * total).astype(BF16)

    def far_copy(sub, i):
        cols = pl.ds(*FAR_SUBS[sub])
        return remote(
            coarse_far.at[mem, :, cols], coarse_far.at[mem, :, cols], e_send.at[sub, i], e_recv.at[sub, i],
            mem_at(MEM_STEPS[i]), space,
        )

    def near_copy(i):
        return remote(
            coarse_near.at[mem], coarse_near.at[mem], n_send.at[i], n_recv.at[i], mem_at(MEM_STEPS[i]), space
        )

    partner = mem_at((0, 1))

    def mid_copy(half, i):
        owner = mem if i < 4 else partner
        target = mem_at(((0, 1), (2, 0), (1, 0), (3, 0), (2, 0), (1, 0), (3, 0))[i])
        return remote(
            coarse_mid.at[half, owner], coarse_mid.at[half, owner], c_send.at[half, i], c_recv.at[half, i], target, space
        )

    far = core * (CELLS - HALO)
    near = (1 - core) * (CELLS - HALO)
    for sub, (cells, width) in enumerate(FAR_SUBS):
        coarse_far[mem, :, cells : cells + width] = pick(far + cells, width)
        for i in range(N_MEM - 1):
            far_copy(sub, i).start()
    for half in range(2):
        coarse_mid[half, mem] = pick(HALO * (half + 1), HALO)
        for i in range(4):
            mid_copy(half, i).start()
    coarse_near[mem] = pick(near, HALO)
    for i in range(N_MEM - 1):
        near_copy(i).start()

    two = modes_two[...].astype(BF16)

    def reduce_cells(pair, first, coarse):
        width = coarse.shape[1]
        for i in range(2):
            pert = ens[2 * pair + i, :, pl.ds(pl.multiple_of(first, TILE), width)]
            prod[pair, i * LEV_PAD : i * LEV_PAD + LEV, 0:width] = pert * coarse
        value = jnp.dot(two, prod[pair, :, 0:width], preferred_element_type=F32).astype(BF16)
        red[pair * ROWS : (pair + 1) * ROWS, pl.ds(pl.multiple_of(HALO + first, TILE), width)] = value

    far_target = lax.rem(space + 2 * core + N_SPACE - 1, N_SPACE)
    far_place = (1 - core) * (HALO + CELLS)

    def far_halo(sub):
        cells, width = FAR_SUBS[sub]
        return remote(
            red.at[:, pl.ds(pl.multiple_of(HALO + far + cells, TILE), width)],
            red.at[:, pl.ds(pl.multiple_of(far_place + cells, TILE), width)],
            f_send.at[sub], f_recv.at[sub], mem, far_target,
        )

    def near_halo(pair):
        rows = pl.ds(pair * ROWS, ROWS)
        return remote(
            red.at[rows, pl.ds(pl.multiple_of(HALO + near, HALO), HALO)],
            red.at[rows, pl.ds(pl.multiple_of(core * (HALO + CELLS), HALO), HALO)],
            h_send.at[pair], h_recv.at[pair], mem, space + 1 - 2 * core,
        )

    loads[3].wait()
    for sub, (cells, width) in enumerate(FAR_SUBS):
        for i in range(N_MEM - 1):
            far_copy(sub, i).wait_recv()
        coarse = coarse_far[:, :, cells : cells + width].reshape(LEV_PAD, width)[0:LEV]
        for pair in range(PAIRS):
            reduce_cells(pair, far + cells, coarse)
        far_halo(sub).start()

    for half in range(2):
        mid_copy(half, 0).wait_recv()
        for i in range(4, N_MEM - 1):
            mid_copy(half, i).start()

    for i in range(N_MEM - 1):
        near_copy(i).wait_recv()
    coarse = coarse_near[...].reshape(LEV_PAD, HALO)[0:LEV]
    for pair in range(PAIRS):
        reduce_cells(pair, near, coarse)
        near_halo(pair).start()

    loads[4].wait()
    done = 0
    for half in range(2):
        for i in range(1, N_MEM - 1):
            mid_copy(half, i).wait_recv()
        coarse = coarse_mid[half].reshape(LEV_PAD, HALO)[0:LEV]
        for pair in range(PAIRS):
            reduce_cells(pair, HALO * (half + 1), coarse)
        for part in range(done, (2, CELLS // PART)[half]):
            cells = part * PART
            low, high = own_rows(cells)
            own[:, cells : cells + PART] = jnp.dot(
                red[:, cells + low : cells + high], paired(stencil, cells, low, high), preferred_element_type=F32
            )
        done = 2

    for k in range(2):
        for i in range(N_MEM - 1):
            level_copy(k, i).wait_send()
        for i in range(counts[k]):
            column_copy(k, i).wait_send()
    for i in range(N_MEM - 1):
        for n in range(2):
            far_copy(n, i).wait_send()
            mid_copy(n, i).wait_send()
        near_copy(i).wait_send()
    for pair in range(PAIRS):
        near_halo(pair).wait()
    for sub in range(2):
        far_halo(sub).wait()


def edge_kernel(halo_rows, ext, own, stencil, out, result, sems):
    mid_copy = pltpu.make_async_copy(own.at[:, pl.ds(HALO, MID)], out.at[:, pl.ds(HALO, MID)], sems.at[0])
    mid_copy.start()
    copies = [mid_copy]

    col = lax.broadcasted_iota(jnp.int32, (16, HALO), 1)
    low_kept = (col >= HALO - halo_rows[0, 0]).astype(F32).astype(BF16)[0:1]
    high_kept = (col < halo_rows[0, 1]).astype(F32).astype(BF16)[0:1]

    for n, part in enumerate((0, 1, CELLS // PART - 2, CELLS // PART - 1)):
        cells = part * PART
        low, high = own_rows(cells)
        if part < 2:
            low, high = 0, low
            kept = low_kept[:, cells:]
        else:
            low, high = high, SPAN
            kept = high_kept[:, 0 : high - low]
        window = ext[:, cells + low : cells + high] * kept
        result[n] = own[:, cells : cells + PART] + jnp.dot(
            window, paired(stencil, cells, low, high), preferred_element_type=F32
        )
        copy = pltpu.make_async_copy(result.at[n], out.at[:, pl.ds(cells, PART)], sems.at[n + 1])
        copy.start()
        copies.append(copy)
    for copy in copies:
        copy.wait()


def local(ens_pert, vert_modes, loc_stencil, grad_hi, child_map, halo_rows):
    vmem = pl.BlockSpec(memory_space=pltpu.VMEM)
    hbm = pl.BlockSpec(memory_space=pltpu.HBM)
    anywhere = pl.BlockSpec(memory_space=pl.ANY)
    dma = pltpu.SemaphoreType.DMA
    held = [
        pltpu.with_memory_space_constraint(x, pltpu.HBM)
        for x in (grad_hi, child_map, vert_modes.T, ens_pert, loc_stencil)
    ]
    ext, own, stencil = pl.pallas_call(
        reduce_kernel,
        out_shape=(
            jax.ShapeDtypeStruct((ALL_ROWS, EXT), BF16),
            jax.ShapeDtypeStruct((ALL_ROWS, CELLS), F32),
            jax.ShapeDtypeStruct((TILE + 2 * HALO, CELLS), BF16),
        ),
        in_specs=[hbm] * 5,
        out_specs=(vmem, vmem, vmem),
        scratch_shapes=[
            pltpu.VMEM((LEV, HI), F32),
            pltpu.VMEM((4, CELLS), jnp.int32),
            pltpu.VMEM((MODES, LEV), BF16),
            pltpu.VMEM((2 * PAIRS, LEV, CELLS), BF16),
            pltpu.VMEM((N_MEM, CHUNK, HI), BF16),
            pltpu.VMEM((N_MEM, CHUNK, HI), BF16),
            pltpu.VMEM((N_SPACE, SEND, LEV_PAD), BF16),
            pltpu.VMEM((N_SPACE, SEND, LEV_PAD), BF16),
            pltpu.VMEM((2 * LEV_PAD, CODES), BF16),
            pltpu.VMEM((CODES, 4 * CELLS), BF16),
            pltpu.VMEM((N_MEM, CHUNK, HALO), BF16),
            pltpu.VMEM((N_MEM, CHUNK, HALO), BF16),
            pltpu.VMEM((2, N_MEM, CHUNK, HALO), BF16),
            pltpu.VMEM((PAIRS, 2 * LEV_PAD, HALO), BF16),
            pltpu.VMEM((ROWS, 2 * LEV_PAD), F32),
            dma((5,)),
            dma((2, N_MEM)),
            dma((2, N_MEM)),
            dma((2, N_SPACE // 2)),
            dma((2, N_SPACE // 2)),
            dma((2, N_MEM)),
            dma((2, N_MEM)),
            dma((N_MEM,)),
            dma((N_MEM,)),
            dma((2, N_MEM)),
            dma((2, N_MEM)),
            dma((2,)),
            dma((2,)),
            dma((PAIRS,)),
            dma((PAIRS,)),
        ],
        compiler_params=pltpu.CompilerParams(
            collective_id=0, has_side_effects=True, vmem_limit_bytes=40 * 2**20
        ),
        name="reduce",
    )(*held)

    out = pl.pallas_call(
        edge_kernel,
        out_shape=jax.ShapeDtypeStruct((ALL_ROWS, CELLS), F32),
        in_specs=[pl.BlockSpec(memory_space=pltpu.SMEM), vmem, vmem, vmem],
        out_specs=anywhere,
        scratch_shapes=[pltpu.VMEM((4, ALL_ROWS, PART), F32), dma((5,))],
        compiler_params=pltpu.CompilerParams(vmem_limit_bytes=40 * 2**20),
        name="edges",
    )(halo_rows.T, ext, own, stencil)
    return out.reshape(2 * PAIRS, MODES, CELLS)


def solution(mesh):
    placed = (
        P("mem", None, "space"),
        P(),
        P(None, "space"),
        P(None, ("mem", "space")),
        P(None, "space"),
        P(None, "space"),
    )
    return jax.shard_map(
        local, mesh=mesh, in_specs=placed, out_specs=P("mem", None, "space"), check_vma=False
    )
```

```python
import jax
import jax.numpy as jnp
from jax import lax
from jax.experimental import pallas as pl
from jax.experimental.pallas import tpu as pltpu
from jax.sharding import PartitionSpec as P

MESH = pl.DeviceIdType.MESH
BF16 = jnp.bfloat16
F32 = jnp.float32

TILE = 128
HALO = 512
LEV = 127
LEV_PAD = 128
MODES = 40
CELLS = 2048
EXT = CELLS + 2 * HALO
N_MEM = 8
N_SPACE = 32
CHUNK = LEV_PAD // N_MEM
HI = 1024
SEND = HI // N_SPACE
CODES = 512
GROUPS = N_MEM * HI // CODES
PAIRS = 5
ROWS = 2 * MODES
ALL_ROWS = PAIRS * ROWS
MID = CELLS - 2 * HALO
FAR_SUBS = ((0, 2 * TILE), (2 * TILE, HALO - 2 * TILE))
PART = 2 * TILE
SPAN = PART + 2 * HALO

MEM_STEPS = ((2, 1), (1, 1), (3, 1), (0, 1), (2, 0), (1, 0), (3, 0))
Z_STEPS = (4, 3, 5, 2, 6, 1, 7, 0)
OWN_STEPS = [(z, c) for z in Z_STEPS for c in (1, 0) if z or c]
OTHER_STEPS = [(z, c) for z in Z_STEPS for c in (1, 0)]


def remote(src, dst, send, recv, mem, space):
    return pltpu.make_async_remote_copy(
        src_ref=src,
        dst_ref=dst,
        send_sem=send,
        recv_sem=recv,
        device_id=(mem, space),
        device_id_type=MESH,
    )


def paired(stencil, cells, low, high):
    depth = TILE + 2 * HALO
    even = [stencil[low : min(high, depth), cells : cells + TILE]]
    if high > depth:
        even.append(jnp.zeros((high - depth, TILE), BF16))
    odd = [stencil[max(low - TILE, 0) : high - TILE, cells + TILE : cells + PART]]
    if low < TILE:
        odd.insert(0, jnp.zeros((TILE - low, TILE), BF16))
    return jnp.concatenate([jnp.concatenate(even, axis=0), jnp.concatenate(odd, axis=0)], axis=1)


def own_rows(cells):
    return max(HALO - cells, 0), min(SPAN, HALO + CELLS - cells)


def reduce_kernel(
    grad_hbm, child_hbm, modes_hbm, ens_hbm, stencil_hbm, red, own, stencil,
    grad, child, modes, ens, gb, got_levels, turned, got_cols, table, picker,
    coarse_far, coarse_near, coarse_mid, prod, modes_two,
    in_sem, m_send, m_recv, s_send, s_recv, e_send, e_recv, n_send, n_recv, c_send, c_recv, f_send, f_recv, h_send, h_recv,
):
    mem = lax.axis_index("mem")
    space = lax.axis_index("space")
    y, x_hi = mem // 2, lax.rem(mem, 2)
    x_lo, z, core = space // 16, lax.rem(space // 2, 8), lax.rem(space, 2)

    def mem_at(step):
        return lax.rem(y + step[0], 4) * 2 + lax.rem(x_hi + step[1], 2)

    def space_at(x, step):
        return x * 16 + lax.rem(z + step[0], 8) * 2 + lax.rem(core + step[1], 2)

    loads = [
        pltpu.make_async_copy(src, dst, in_sem.at[i])
        for i, (src, dst) in enumerate(
            (
                (grad_hbm, grad),
                (modes_hbm, modes),
                (child_hbm, child),
                (ens_hbm, ens),
                (stencil_hbm, stencil),
            )
        )
    ]
    loads[0].start()

    barrier = pltpu.get_barrier_semaphore()
    for step in OTHER_STEPS:
        pl.semaphore_signal(barrier, inc=1, device_id=(mem, space_at(1 - x_lo, step)), device_id_type=MESH)
    for step in MEM_STEPS:
        pl.semaphore_signal(barrier, inc=1, device_id=(mem_at(step), space), device_id_type=MESH)
    for step in OWN_STEPS:
        pl.semaphore_signal(barrier, inc=1, device_id=(mem, space_at(x_lo, step)), device_id_type=MESH)

    loads[0].wait()
    for m in range(N_MEM - 1):
        gb[m] = grad[m * CHUNK : (m + 1) * CHUNK, :].astype(BF16)
    last = grad[(N_MEM - 1) * CHUNK : LEV, :]
    gb[N_MEM - 1] = jnp.concatenate([last, jnp.zeros((1, HI), F32)], axis=0).astype(BF16)

    pl.semaphore_wait(barrier, N_MEM - 1 + N_SPACE - 1)

    sides = (1 - x_lo, x_lo)

    def level_copy(k, i):
        target = mem_at(MEM_STEPS[i])
        cols = pl.ds(pl.multiple_of(sides[k] * CODES, CODES), CODES)
        return remote(
            gb.at[target, :, cols], got_levels.at[mem, :, cols], m_send.at[k, i], m_recv.at[k, i], target, space
        )

    for k in range(2):
        for i in range(N_MEM - 1):
            level_copy(k, i).start()
    for load in loads[1:]:
        load.start()

    got_levels[mem] = gb[mem]

    loads[1].wait()
    modes_two[...] = jnp.zeros_like(modes_two)
    wide = modes[...].astype(F32)
    modes_two[0:MODES, 0:LEV] = wide
    modes_two[MODES:ROWS, LEV_PAD : LEV_PAD + LEV] = wide
    prod[...] = jnp.zeros_like(prod)

    def column_copy(k, i):
        target = space_at(sides[k], (OTHER_STEPS, OWN_STEPS)[k][i])
        return remote(turned.at[target], got_cols.at[space], s_send.at[k, i], s_recv.at[k, i], mem, target)

    counts = (len(OTHER_STEPS), len(OWN_STEPS))
    for k in range(2):
        for i in range(N_MEM - 1):
            level_copy(k, i).wait_recv()
        for q in range(CODES // 128):
            first = pl.multiple_of(sides[k] * CODES + q * 128, 128)
            part = got_levels[:, :, pl.ds(first, 128)].reshape(LEV_PAD, 128)
            turned[pl.ds(sides[k] * 16 + q * 4, 4)] = part.T.reshape(4, SEND, LEV_PAD)
        for i in range(counts[k]):
            column_copy(k, i).start()

    got_cols[space] = turned[space]
    loads[2].wait()

    @pl.loop(0, 4 * CELLS // 256)
    def _(t):
        j = t // (CELLS // 256)
        first = pl.multiple_of(lax.rem(t, CELLS // 256) * 256, 256)
        low = child[pl.ds(j, 1), pl.ds(first, 256)] & (CODES - 1)
        hot = lax.broadcasted_iota(jnp.int32, (CODES, 256), 0) == low
        picker[:, pl.ds(pl.multiple_of(t * 256, 256), 256)] = hot.astype(F32).astype(BF16)

    for k in range(2):
        for i in range(counts[k]):
            column_copy(k, i).wait_recv()
        cols = got_cols[pl.ds(sides[k] * 16, 16)].reshape(CODES, LEV_PAD)
        table[pl.ds(pl.multiple_of(sides[k] * LEV_PAD, LEV_PAD), LEV_PAD), :] = cols.T

    def pick(first, width):
        total = jnp.zeros((CHUNK, width), F32)
        for j in range(4):
            cells = pl.ds(pl.multiple_of(j * CELLS + first, TILE), width)
            found = jnp.dot(table[...], picker[:, cells], preferred_element_type=F32)
            code = child[j : j + 1, pl.ds(pl.multiple_of(first, TILE), width)]
            group = ((code >> 9) & 1) * N_MEM + (code >> 10)
            for g in range(GROUPS):
                total = total + jnp.where(group == g, found[g * CHUNK : (g + 1) * CHUNK, :], 0.0)
        return (0.25 * total).astype(BF16)

    def far_copy(sub, i):
        cols = pl.ds(*FAR_SUBS[sub])
        target = i + (mem <= i).astype(jnp.int32)
        return remote(
            coarse_far.at[mem, :, cols], coarse_far.at[mem, :, cols], e_send.at[sub, i], e_recv.at[sub, mem],
            target, space,
        )

    def far_arrived(sub, d):
        cols = pl.ds(*FAR_SUBS[sub])
        source = lax.rem(mem + d, N_MEM)
        return remote(
            coarse_far.at[source, :, cols], coarse_far.at[source, :, cols], e_send.at[sub, 0], e_recv.at[sub, source],
            source, space,
        )

    def near_copy(i):
        return remote(
            coarse_near.at[mem], coarse_near.at[mem], n_send.at[i], n_recv.at[i], mem_at(MEM_STEPS[i]), space
        )

    partner = mem_at((0, 1))

    def mid_copy(half, i):
        owner = mem if i < 4 else partner
        target = mem_at(((0, 1), (2, 0), (1, 0), (3, 0), (2, 0), (1, 0), (3, 0))[i])
        return remote(
            coarse_mid.at[half, owner], coarse_mid.at[half, owner], c_send.at[half, i], c_recv.at[half, i], target, space
        )

    far = core * (CELLS - HALO)
    near = (1 - core) * (CELLS - HALO)
    for sub, (cells, width) in enumerate(FAR_SUBS):
        coarse_far[mem, :, cells : cells + width] = pick(far + cells, width)
        for i in range(N_MEM - 1):
            far_copy(sub, i).start()
    for half in range(2):
        coarse_mid[half, mem] = pick(HALO * (half + 1), HALO)
        for i in range(4):
            mid_copy(half, i).start()
    coarse_near[mem] = pick(near, HALO)
    for i in range(N_MEM - 1):
        near_copy(i).start()

    two = modes_two[...].astype(BF16)

    def reduce_cells(pair, first, coarse):
        width = coarse.shape[1]
        for i in range(2):
            pert = ens[2 * pair + i, :, pl.ds(pl.multiple_of(first, TILE), width)]
            prod[pair, i * LEV_PAD : i * LEV_PAD + LEV, 0:width] = pert * coarse
        value = jnp.dot(two, prod[pair, :, 0:width], preferred_element_type=F32).astype(BF16)
        red[pair * ROWS : (pair + 1) * ROWS, pl.ds(pl.multiple_of(HALO + first, TILE), width)] = value

    far_target = lax.rem(space + 2 * core + N_SPACE - 1, N_SPACE)
    far_place = (1 - core) * (HALO + CELLS)

    def far_halo(sub):
        cells, width = FAR_SUBS[sub]
        return remote(
            red.at[:, pl.ds(pl.multiple_of(HALO + far + cells, TILE), width)],
            red.at[:, pl.ds(pl.multiple_of(far_place + cells, TILE), width)],
            f_send.at[sub], f_recv.at[sub], mem, far_target,
        )

    def near_halo(pair):
        rows = pl.ds(pair * ROWS, ROWS)
        return remote(
            red.at[rows, pl.ds(pl.multiple_of(HALO + near, HALO), HALO)],
            red.at[rows, pl.ds(pl.multiple_of(core * (HALO + CELLS), HALO), HALO)],
            h_send.at[pair], h_recv.at[pair], mem, space + 1 - 2 * core,
        )

    loads[3].wait()
    for sub, (cells, width) in enumerate(FAR_SUBS):
        for i in range(N_MEM - 1):
            far_arrived(sub, i + 1).wait_recv()
        coarse = coarse_far[:, :, cells : cells + width].reshape(LEV_PAD, width)[0:LEV]
        for pair in range(PAIRS):
            reduce_cells(pair, far + cells, coarse)
        far_halo(sub).start()

    for half in range(2):
        mid_copy(half, 0).wait_recv()
        for i in range(4, N_MEM - 1):
            mid_copy(half, i).start()

    for i in range(N_MEM - 1):
        near_copy(i).wait_recv()
    coarse = coarse_near[...].reshape(LEV_PAD, HALO)[0:LEV]
    for pair in range(PAIRS):
        reduce_cells(pair, near, coarse)
        near_halo(pair).start()

    loads[4].wait()
    done = 0
    for half in range(2):
        for i in range(1, N_MEM - 1):
            mid_copy(half, i).wait_recv()
        coarse = coarse_mid[half].reshape(LEV_PAD, HALO)[0:LEV]
        for pair in range(PAIRS):
            reduce_cells(pair, HALO * (half + 1), coarse)
        for part in range(done, (2, CELLS // PART)[half]):
            cells = part * PART
            low, high = own_rows(cells)
            own[:, cells : cells + PART] = jnp.dot(
                red[:, cells + low : cells + high], paired(stencil, cells, low, high), preferred_element_type=F32
            )
        done = 2

    for k in range(2):
        for i in range(N_MEM - 1):
            level_copy(k, i).wait_send()
        for i in range(counts[k]):
            column_copy(k, i).wait_send()
    for i in range(N_MEM - 1):
        for n in range(2):
            far_copy(n, i).wait_send()
            mid_copy(n, i).wait_send()
        near_copy(i).wait_send()
    for pair in range(PAIRS):
        near_halo(pair).wait()
    for sub in range(2):
        far_halo(sub).wait()


def edge_kernel(halo_rows, ext, own, stencil, out, result, sems):
    mid_copy = pltpu.make_async_copy(own.at[:, pl.ds(HALO, MID)], out.at[:, pl.ds(HALO, MID)], sems.at[0])
    mid_copy.start()
    copies = [mid_copy]

    col = lax.broadcasted_iota(jnp.int32, (16, HALO), 1)
    low_kept = (col >= HALO - halo_rows[0, 0]).astype(F32).astype(BF16)[0:1]
    high_kept = (col < halo_rows[0, 1]).astype(F32).astype(BF16)[0:1]

    for n, part in enumerate((0, 1, CELLS // PART - 2, CELLS // PART - 1)):
        cells = part * PART
        low, high = own_rows(cells)
        if part < 2:
            low, high = 0, low
            kept = low_kept[:, cells:]
        else:
            low, high = high, SPAN
            kept = high_kept[:, 0 : high - low]
        window = ext[:, cells + low : cells + high] * kept
        result[n] = own[:, cells : cells + PART] + jnp.dot(
            window, paired(stencil, cells, low, high), preferred_element_type=F32
        )
        copy = pltpu.make_async_copy(result.at[n], out.at[:, pl.ds(cells, PART)], sems.at[n + 1])
        copy.start()
        copies.append(copy)
    for copy in copies:
        copy.wait()


def local(ens_pert, vert_modes, loc_stencil, grad_hi, child_map, halo_rows):
    vmem = pl.BlockSpec(memory_space=pltpu.VMEM)
    hbm = pl.BlockSpec(memory_space=pltpu.HBM)
    anywhere = pl.BlockSpec(memory_space=pl.ANY)
    dma = pltpu.SemaphoreType.DMA
    held = [
        pltpu.with_memory_space_constraint(x, pltpu.HBM)
        for x in (grad_hi, child_map, vert_modes.T, ens_pert, loc_stencil)
    ]
    ext, own, stencil = pl.pallas_call(
        reduce_kernel,
        out_shape=(
            jax.ShapeDtypeStruct((ALL_ROWS, EXT), BF16),
            jax.ShapeDtypeStruct((ALL_ROWS, CELLS), F32),
            jax.ShapeDtypeStruct((TILE + 2 * HALO, CELLS), BF16),
        ),
        in_specs=[hbm] * 5,
        out_specs=(vmem, vmem, vmem),
        scratch_shapes=[
            pltpu.VMEM((LEV, HI), F32),
            pltpu.VMEM((4, CELLS), jnp.int32),
            pltpu.VMEM((MODES, LEV), BF16),
            pltpu.VMEM((2 * PAIRS, LEV, CELLS), BF16),
            pltpu.VMEM((N_MEM, CHUNK, HI), BF16),
            pltpu.VMEM((N_MEM, CHUNK, HI), BF16),
            pltpu.VMEM((N_SPACE, SEND, LEV_PAD), BF16),
            pltpu.VMEM((N_SPACE, SEND, LEV_PAD), BF16),
            pltpu.VMEM((2 * LEV_PAD, CODES), BF16),
            pltpu.VMEM((CODES, 4 * CELLS), BF16),
            pltpu.VMEM((N_MEM, CHUNK, HALO), BF16),
            pltpu.VMEM((N_MEM, CHUNK, HALO), BF16),
            pltpu.VMEM((2, N_MEM, CHUNK, HALO), BF16),
            pltpu.VMEM((PAIRS, 2 * LEV_PAD, HALO), BF16),
            pltpu.VMEM((ROWS, 2 * LEV_PAD), F32),
            dma((5,)),
            dma((2, N_MEM)),
            dma((2, N_MEM)),
            dma((2, N_SPACE // 2)),
            dma((2, N_SPACE // 2)),
            dma((2, N_MEM)),
            dma((2, N_MEM)),
            dma((N_MEM,)),
            dma((N_MEM,)),
            dma((2, N_MEM)),
            dma((2, N_MEM)),
            dma((2,)),
            dma((2,)),
            dma((PAIRS,)),
            dma((PAIRS,)),
        ],
        compiler_params=pltpu.CompilerParams(
            collective_id=0, has_side_effects=True, vmem_limit_bytes=40 * 2**20
        ),
        name="reduce",
    )(*held)

    out = pl.pallas_call(
        edge_kernel,
        out_shape=jax.ShapeDtypeStruct((ALL_ROWS, CELLS), F32),
        in_specs=[pl.BlockSpec(memory_space=pltpu.SMEM), vmem, vmem, vmem],
        out_specs=anywhere,
        scratch_shapes=[pltpu.VMEM((4, ALL_ROWS, PART), F32), dma((5,))],
        compiler_params=pltpu.CompilerParams(vmem_limit_bytes=40 * 2**20),
        name="edges",
    )(halo_rows.T, ext, own, stencil)
    return out.reshape(2 * PAIRS, MODES, CELLS)


def solution(mesh):
    placed = (
        P("mem", None, "space"),
        P(),
        P(None, "space"),
        P(None, ("mem", "space")),
        P(None, "space"),
        P(None, "space"),
    )
    return jax.shard_map(
        local, mesh=mesh, in_specs=placed, out_specs=P("mem", None, "space"), check_vma=False
    )
```
